32 devices in a mesh: node: 16 (over z, y, core), rep: 2 (over x).
Axes of the slice: x: 2, y: 2, z: 4, core: 2. Of those that a mesh axis runs over, the one named last changes fastest.
Arguments:
- node_feats: bfloat16 [4096, 256], P(('node', 'rep')), may hold values from -6 to 6
- tile_vals: bfloat16 [16, 2, 16, 2, 128, 128], P('node', 'rep'), may hold values from -0.125 to 0.125
- tile_rows: int32 [16, 2, 16, 2], P('node', 'rep'), may hold values from 0 to 1
- tile_count: int32 [16, 2, 16], P('node', 'rep'), may hold values from 0 to 2, as said below
- w_self: bfloat16 [256, 256], replicated, may hold values from -0.375 to 0.375
- w_neigh: bfloat16 [256, 256], replicated, may hold values from -0.375 to 0.375
- out_grad: bfloat16 [4096, 256], P(('node', 'rep')), may hold values from -0.09375 to 0.09375
Outputs:
- layer_out: bfloat16 [4096, 256], P(('node', 'rep'))
- grad_self: float32 [256, 256], replicated
- grad_neigh: float32 [256, 256], replicated
The draws below stay inside these ranges and needn't reach their ends.
Inputs may be any that keep to these rules, and one draw needn't show every extreme that they name: `tile_count`: number of live slots of a column block in one device's tile list; every device has a column block with 2 live slots.
All inputs are finite; a program needn't handle non-finite values.
Results may differ from the reference program's by a relative error of at most 0.0055.
Values may be sent and summed in bfloat16 or wider, within the bound.
No kernel may reach another device: no remote copies, remote signals or barrier semaphores. Data moves between devices by JAX's collectives and lax.ppermute only.
A program may use at most 64 MiB of HBM per device.

```python
import math
import jax
import jax.numpy as jnp
from jax import lax

FEAT = 256
HIDDEN_WIDTH = 256
TILE = 128
SLOT = 2
NODES = 4096
N_NODE = 16
N_REP = 2


def draw_tile_count(key, part):
    key = jax.random.fold_in(key, 11)
    key_level, key_raw, key_full = jax.random.split(key, 3)
    level = jax.random.randint(key_level, (N_NODE, N_REP, 1), 1, SLOT + 1)
    raw_count = jax.random.randint(key_raw, (N_NODE, N_REP, N_NODE), 0, 2 * SLOT + 1)
    counts = jnp.minimum(raw_count, level)
    full_col = jax.random.randint(key_full, (N_NODE, N_REP, 1), 0, N_NODE)
    column = jnp.arange(N_NODE, dtype=jnp.int32)[None, None, :]
    return jnp.where(column == full_col, SLOT, counts).astype(jnp.int32)


def place_ends(result, stream_key, least, largest):
    dims = result.shape
    place = [jax.random.randint(jax.random.fold_in(stream_key, axis), (), 0, dims[axis]) for axis in range(len(dims))]
    result = result.at[tuple(place)].set(least)
    longest = dims.index(max(dims))
    place[longest] = (place[longest] + 1) % dims[longest]
    return result.at[tuple(place)].set(largest)


def shard_levels(own_key, dims, cuts, smallest, largest):
    loudness, own = 1.0, jax.random.fold_in(own_key, 6)
    for position, blocks in cuts:
        draws = jnp.exp(jax.random.uniform(jax.random.fold_in(own, position), (blocks,), jnp.float32, smallest / len(cuts), largest / len(cuts)))
        loudness = loudness * jnp.repeat(draws, dims[position] // blocks).reshape([-1 if axis == position else 1 for axis in range(len(dims))])
    return loudness


def bell_draw(key, shape, spread, limit, cuts=(), kind=jnp.bfloat16):
    level = shard_levels(key, shape, cuts, -0.22, 0.18) if cuts else 1.0
    values = jax.random.normal(key, shape, jnp.float32) * spread * level
    return jnp.minimum(jnp.maximum(values, -limit), limit).astype(kind)


def setup_inputs(seed: int = 0) -> dict:
    streams_of = jax.random.split(jax.random.key(seed), 8)
    node_feats = bell_draw(streams_of[0], (NODES, FEAT), 1.0, 6.0, ((0, 32),))
    tile_vals = bell_draw(streams_of[1], (N_NODE, N_REP, N_NODE, SLOT, TILE, TILE), (TILE * N_NODE) ** -0.5, 0.125, ((0, 16), (1, 2)))
    tile_rows = place_ends(jax.random.randint(streams_of[2], (N_NODE, N_REP, N_NODE, SLOT), 0, N_REP), jax.random.fold_in(streams_of[2], 1), 0, N_REP - 1).astype(jnp.int32)
    tile_count = draw_tile_count(jax.random.fold_in(streams_of[7], 71), 0)
    w_self = bell_draw(streams_of[4], (FEAT, HIDDEN_WIDTH), FEAT ** -0.5, 0.375)
    w_neigh = bell_draw(streams_of[5], (FEAT, HIDDEN_WIDTH), FEAT ** -0.5, 0.375)
    out_grad = bell_draw(streams_of[6], (NODES, HIDDEN_WIDTH), (TILE * N_NODE * N_REP) ** -0.5, 0.09375, ((0, 32),))
    return dict(node_feats=node_feats, tile_vals=tile_vals, tile_rows=tile_rows, tile_count=tile_count, w_self=w_self, w_neigh=w_neigh, out_grad=out_grad)


def live_weights(row_ids, live_count, panel_tiles):
    slot_position = jnp.arange(row_ids.shape[1], dtype=jnp.int32)
    target = jnp.arange(panel_tiles, dtype=jnp.int32)
    chosen = row_ids[:, :, None] == target[None, None, :]
    active = slot_position[None, :, None] < live_count[:, None, None]
    return jnp.where(chosen & active, 1.0, 0.0).astype(jnp.float32)


def column_terms(tile_collection, row_ids, live_count, columns, panel_tiles):
    ncols = tile_collection.shape[0]
    group = math.gcd(ncols, 8)
    nsteps = ncols // group
    tile_grp = tile_collection.reshape((nsteps, group) + tile_collection.shape[1:])
    row_grp = row_ids.reshape((nsteps, group) + row_ids.shape[1:])
    count_grp = live_count.reshape((nsteps, group))
    col_grp = columns.reshape((nsteps, group) + columns.shape[1:])

    def one_group(running, inputs):
        tile_block, row_blk, count_blk, column_block = inputs
        product_terms = jnp.einsum('lhjz,lzd->lhjd', tile_block.astype(jnp.float32), column_block.astype(jnp.float32), precision=lax.Precision.HIGHEST)
        weights = live_weights(row_blk, count_blk, panel_tiles)
        return running + jnp.einsum('csr,csaf->raf', weights, product_terms, precision=lax.Precision.HIGHEST), None

    start_sum = jnp.zeros((panel_tiles, tile_collection.shape[2], columns.shape[2]), jnp.float32)
    running, unused = lax.scan(one_group, start_sum, (tile_grp, row_grp, count_grp, col_grp))
    return running


def reference(node_feats, tile_vals, tile_rows, tile_count, w_self, w_neigh, out_grad):
    blocks = node_feats.reshape(N_NODE, N_REP, TILE, FEAT)

    def one_panel(panel_position):
        def one_residue(residue):
            return column_terms(tile_vals[panel_position, residue], tile_rows[panel_position, residue], tile_count[panel_position, residue], blocks[:, residue], N_REP)
        partials = lax.map(one_residue, jnp.arange(N_REP, dtype=jnp.int32))
        return jnp.sum(partials, axis=0)

    panels = lax.map(one_panel, jnp.arange(N_NODE, dtype=jnp.int32))
    aggregate = panels.reshape(N_NODE * N_REP * TILE, FEAT).astype(jnp.bfloat16)
    pre = jnp.dot(node_feats, w_self, preferred_element_type=jnp.float32) + jnp.dot(aggregate, w_neigh, preferred_element_type=jnp.float32)
    sigma = jax.nn.sigmoid(pre)
    layer_out = (pre * sigma).astype(jnp.bfloat16)
    delta = (out_grad.astype(jnp.float32) * sigma * (1.0 + pre * (1.0 - sigma))).astype(jnp.bfloat16)
    grad_self = lax.dot_general(node_feats, delta, (((0,), (0,)), ((), ())), preferred_element_type=jnp.float32)
    grad_neigh = lax.dot_general(aggregate, delta, (((0,), (0,)), ((), ())), preferred_element_type=jnp.float32)
    return layer_out, grad_self, grad_neigh
```

```python
import functools

import jax
import jax.numpy as jnp
from jax import lax
from jax.experimental import pallas as pl
from jax.experimental.pallas import tpu as pltpu
from jax.sharding import PartitionSpec as P

VMEM = pl.BlockSpec(memory_space=pltpu.VMEM)
SMEM = pl.BlockSpec(memory_space=pltpu.SMEM)
F32 = jnp.float32
BF16 = jnp.bfloat16


def bits_below(size):
    return [1 << i for i in reversed(range(size.bit_length() - 1))]


def doubling_masks(bits):
    masks = [0]
    for bit in bits:
        masks = masks + [mask ^ bit for mask in masks]
    return masks


def swap(x, n_node, n_rep, even, odd):
    pairs = []
    for node in range(n_node):
        flip_node, flip_rep = odd if node & 1 else even
        for rep in range(n_rep):
            pairs.append((node * n_rep + rep, (node ^ flip_node) * n_rep + (rep ^ flip_rep)))
    return lax.ppermute(x, ("node", "rep"), pairs)


def tile_sums(masks_even, masks_odd, other_core, seeded, *refs):
    if seeded:
        place, rows, count, tiles, columns, seed, out = refs
    else:
        place, rows, count, tiles, columns, out = refs
    node, rep = place[0], place[1]
    n_blocks = len(masks_even)
    tile = tiles.shape[2]
    panel_tiles = out.shape[0] // tile
    slots = tiles.shape[1]
    core = node & 1
    origin = node ^ 1 if other_core else node
    swapped = core == (1 if not other_core else 0)

    def pair_terms(step, even, odd):
        groups = [origin ^ even, origin ^ odd]
        block = columns[pl.ds(pl.multiple_of(step * 2 * tile, 2 * tile), 2 * tile), :]
        for k in range(panel_tiles):
            target = rep ^ k
            total = None
            for s in range(slots):
                parts = []
                for group in groups:
                    live = jnp.logical_and(s < count[group], rows[group * slots + s] == target)
                    weight = jnp.where(live, 1.0, 0.0).astype(F32)
                    value = tiles[group, s]
                    parts.append(jnp.where(jnp.full(value.shape, weight) > 0.5, value, jnp.zeros_like(value)))
                left = jnp.concatenate(parts, axis=1)
                term = jnp.dot(left, block, preferred_element_type=F32)
                total = term if total is None else total + term
            out[k * tile : (k + 1) * tile, :] += total

    out[...] = seed[...] if seeded else jnp.zeros_like(out)
    for step in range(n_blocks // 2):
        pair = [
            jnp.where(swapped, masks_odd[2 * step + i], masks_even[2 * step + i]) for i in (0, 1)
        ]
        pair_terms(step, pair[0], pair[1])


def update(own, got, feats, w_self, w_neigh, out_grad, layer_out, send):
    aggregate = (own[...] + got[...].astype(F32)).astype(BF16)
    pre = jnp.dot(feats[...], w_self[...], preferred_element_type=F32) + jnp.dot(
        aggregate, w_neigh[...], preferred_element_type=F32
    )
    sigma = jax.nn.sigmoid(pre)
    layer_out[...] = (pre * sigma).astype(BF16)
    delta = (out_grad[...].astype(F32) * sigma * (1.0 + pre * (1.0 - sigma))).astype(BF16)
    rows = feats.shape[0]
    send[:rows, :] = delta
    send[rows:, :] = aggregate


def chip_gradient(place, feats, other_feats, mine, other, out):
    rows = feats.shape[0]
    first = jnp.full(feats.shape, place[0] & 1) == 0
    left = jnp.concatenate(
        [
            jnp.where(first, feats[...], mine[rows:, :]),
            jnp.where(first, other_feats[:rows, :], other[rows:, :]),
        ],
        axis=0,
    )
    delta = jnp.concatenate([mine[:rows, :], other[:rows, :]], axis=0)
    out[...] = lax.dot_general(
        left, delta, (((0,), (0,)), ((), ())), preferred_element_type=F32
    ).astype(out.dtype)


def call(body, out_shape, specs, flops, nbytes):
    return pl.pallas_call(
        body,
        out_shape=out_shape,
        in_specs=specs,
        out_specs=jax.tree.map(lambda _: VMEM, out_shape),
        cost_estimate=pl.CostEstimate(flops=flops, bytes_accessed=nbytes, transcendentals=0),
        compiler_params=pltpu.CompilerParams(vmem_limit_bytes=24 * 1024 * 1024),
    )


def local(n_node, n_rep, node_feats, tile_vals, tile_rows, tile_count, w_self, w_neigh, out_grad):
    tiles = tile_vals[0, 0]
    row_ids = tile_rows[0, 0].reshape(-1)
    live_count = tile_count[0, 0]
    rows, width = node_feats.shape
    place = jnp.stack([lax.axis_index("node"), lax.axis_index("rep")]).astype(jnp.int32)

    chip_bits = bits_below(n_node)[:-1]
    turned = chip_bits[-1:] + chip_bits[:-1]
    rep_bits = bits_below(n_rep)

    held = node_feats
    for even, odd in zip(chip_bits, turned, strict=True):
        held = jnp.concatenate([held, swap(held, n_node, n_rep, (even, 0), (odd, 0))], axis=0)
    other_held = swap(held, n_node, n_rep, (1, 0), (1, 0))

    masks_even, masks_odd = doubling_masks(chip_bits), doubling_masks(turned)
    panel = jax.ShapeDtypeStruct((n_rep * rows, width), F32)
    flops = held.shape[0] * n_rep * rows * width * 4
    nbytes = tiles.size + held.size * 2 + panel.size * 4
    own = call(
        functools.partial(tile_sums, masks_even, masks_odd, False, False),
        panel, [SMEM] * 3 + [VMEM] * 2, flops, nbytes,
    )(place, row_ids, live_count, tiles, held)
    total = call(
        functools.partial(tile_sums, masks_even, masks_odd, True, True),
        panel, [SMEM] * 3 + [VMEM] * 3, flops, nbytes,
    )(place, row_ids, live_count, tiles, other_held, own)

    for bit in rep_bits[:-1]:
        half = bit * rows
        got = swap(total[half:].astype(BF16), n_node, n_rep, (0, bit), (0, bit))
        total = total[:half] + got.astype(F32)
    got = swap(total[rows:].astype(BF16), n_node, n_rep, (0, 1), (0, 1))

    layer_out, mine = call(
        update,
        (jax.ShapeDtypeStruct((rows, width), BF16), jax.ShapeDtypeStruct((2 * rows, width), BF16)),
        [VMEM] * 6, 4 * rows * width * width, 1 << 20,
    )(total[:rows], got, node_feats, w_self, w_neigh, out_grad)
    other = swap(mine, n_node, n_rep, (1, 0), (1, 0))
    grad = call(
        chip_gradient, jax.ShapeDtypeStruct((width, width), BF16),
        [SMEM] + [VMEM] * 4, 4 * rows * width * width, 1 << 20,
    )(place, node_feats, other_held[:rows], mine, other)

    steps = [(0, bit) for bit in rep_bits] + [(bit, 0) for bit in reversed(chip_bits)]
    half = len(rep_bits) + 1
    first, rest = steps[:half], steps[half:]
    order_even = first + rest
    order_odd = first[::-1] + rest[::-1]
    for even, odd in zip(order_even, order_odd, strict=True):
        got = swap(grad.astype(BF16), n_node, n_rep, even, odd)
        grad = grad.astype(BF16).astype(F32) + got.astype(F32)
    other_grad = swap(grad, n_node, n_rep, (1, 0), (1, 0))
    first_core = (place[0] & 1) == 0
    grad_self = jnp.where(first_core, grad, other_grad)
    grad_neigh = jnp.where(first_core, other_grad, grad)
    return (layer_out, grad_self, grad_neigh)


def solution(mesh):
    placed = (
        P(("node", "rep"), None),
        P("node", "rep", None, None, None, None),
        P("node", "rep", None, None),
        P("node", "rep", None),
        P(),
        P(),
        P(("node", "rep"), None),
    )
    return jax.shard_map(
        functools.partial(local, mesh.shape["node"], mesh.shape["rep"]),
        mesh=mesh,
        in_specs=placed,
        out_specs=(P(("node", "rep"), None), P(), P()),
        check_vma=False,
    )
```

```python
import functools

import jax
import jax.numpy as jnp
from jax import lax
from jax.experimental import pallas as pl
from jax.experimental.pallas import tpu as pltpu
from jax.sharding import PartitionSpec as P

VMEM = pl.BlockSpec(memory_space=pltpu.VMEM)
SMEM = pl.BlockSpec(memory_space=pltpu.SMEM)
F32 = jnp.float32
BF16 = jnp.bfloat16


def bits_below(size):
    return [1 << i for i in reversed(range(size.bit_length() - 1))]


def doubling_masks(bits):
    masks = [0]
    for bit in bits:
        masks = masks + [mask ^ bit for mask in masks]
    return masks


def swap(x, n_node, n_rep, even, odd):
    pairs = []
    for node in range(n_node):
        flip_node, flip_rep = odd if node & 1 else even
        for rep in range(n_rep):
            pairs.append((node * n_rep + rep, (node ^ flip_node) * n_rep + (rep ^ flip_rep)))
    return lax.ppermute(x, ("node", "rep"), pairs)


def tile_sums(masks_even, masks_odd, other_core, seeded, *refs):
    if seeded:
        place, rows, count, tiles, columns, seed, out = refs
    else:
        place, rows, count, tiles, columns, out = refs
    node = place[0]
    base = place[1] - lax.rem(place[1], 2)
    tile = tiles.shape[2]
    panel_tiles = out.shape[0] // tile
    slots = tiles.shape[1]
    origin = node ^ 1 if other_core else node
    odd = (origin & 1) == 1

    total = seed[...] if seeded else None
    for step in range(len(masks_even) // 2):
        groups = [
            origin ^ jnp.where(odd, masks_odd[2 * step + i], masks_even[2 * step + i]) for i in (0, 1)
        ]
        lefts = []
        for s in range(slots):
            for k in range(panel_tiles):
                parts = []
                for group in groups:
                    live = jnp.logical_and(s < count[group], rows[group * slots + s] == base ^ k)
                    value = tiles[group, s]
                    chosen = jnp.full(value.shape, live.astype(F32)) > 0.5
                    parts.append(jnp.where(chosen, value, jnp.zeros_like(value)))
                lefts.append(jnp.concatenate(parts, axis=1))
        block = columns[step * 2 * tile : (step + 1) * 2 * tile, :]
        terms = jnp.dot(jnp.concatenate(lefts, axis=0), block, preferred_element_type=F32)
        for s in range(slots):
            term = terms[s * panel_tiles * tile : (s + 1) * panel_tiles * tile]
            total = term if total is None else total + term
    out[...] = total.astype(out.dtype)


def update(place, own, got, feats, far_feats, out_grad, far_out_grad, w_self, w_neigh, layer_out, keep, send):
    rows = feats.shape[0]
    first_rep = jnp.full((rows, feats.shape[1]), lax.rem(place[1], 2)) == 0

    def in_order(mine, far):
        return jnp.concatenate([jnp.where(first_rep, mine, far), jnp.where(first_rep, far, mine)], axis=0)

    x = in_order(feats[...], far_feats[...])
    g = in_order(out_grad[...], far_out_grad[...]).astype(F32)
    aggregate = (own[...].astype(F32) + got[...].astype(F32)).astype(BF16)
    pre = jnp.dot(x, w_self[...], preferred_element_type=F32) + jnp.dot(
        aggregate, w_neigh[...], preferred_element_type=F32
    )
    sigma = jax.nn.sigmoid(pre)
    value = (pre * sigma).astype(BF16)
    layer_out[...] = jnp.where(first_rep, value[:rows], value[rows:])
    delta = (g * sigma * (1.0 + pre * (1.0 - sigma))).astype(BF16)
    first_core = jnp.full(x.shape, place[0] & 1) == 0
    for left, out in ((jnp.where(first_core, x, aggregate), keep), (jnp.where(first_core, aggregate, x), send)):
        out[...] = lax.dot_general(
            left, delta, (((0,), (0,)), ((), ())), preferred_element_type=F32
        ).astype(out.dtype)


def copied(x_ref, out_ref):
    out_ref[...] = x_ref[...]


def call(body, out_shape, specs, flops, nbytes):
    return pl.pallas_call(
        body,
        out_shape=out_shape,
        in_specs=specs,
        out_specs=jax.tree.map(lambda _: VMEM, out_shape),
        cost_estimate=pl.CostEstimate(flops=flops, bytes_accessed=nbytes, transcendentals=0),
        compiler_params=pltpu.CompilerParams(vmem_limit_bytes=24 * 1024 * 1024),
    )


def local(n_node, n_rep, node_feats, tile_vals, tile_rows, tile_count, w_self, w_neigh, out_grad):
    tiles = tile_vals[0, 0]
    row_ids = tile_rows[0, 0].reshape(-1)
    live_count = tile_count[0, 0]
    rows, width = node_feats.shape
    place = jnp.stack([lax.axis_index("node"), lax.axis_index("rep")]).astype(jnp.int32)

    chip_bits = bits_below(n_node)[:-1]
    turned = chip_bits[-1:] + chip_bits[:-1]
    rep_bits = bits_below(n_rep)

    got = swap(node_feats, n_node, n_rep, (chip_bits[0], 0), (turned[0], 0))
    feats = call(copied, jax.ShapeDtypeStruct(node_feats.shape, BF16), [VMEM], 0, node_feats.size * 4)(node_feats)
    feats, got, place, row_ids, live_count = lax.optimization_barrier((feats, got, place, row_ids, live_count))
    held = jnp.concatenate([feats, got], axis=0)
    far = swap(jnp.concatenate([feats, out_grad], axis=0), n_node, n_rep, (0, 1), (0, 1))
    for even, odd in zip(chip_bits[1:], turned[1:], strict=True):
        held = jnp.concatenate([held, swap(held, n_node, n_rep, (even, 0), (odd, 0))], axis=0)
    other_held = swap(held, n_node, n_rep, (1, 0), (1, 0))

    masks_even, masks_odd = doubling_masks(chip_bits), doubling_masks(turned)
    flops = held.shape[0] * n_rep * rows * width * 4
    nbytes = tiles.size + held.size * 2 + n_rep * rows * width * 4
    own = call(
        functools.partial(tile_sums, masks_even, masks_odd, False, False),
        jax.ShapeDtypeStruct((n_rep * rows, width), F32), [SMEM] * 3 + [VMEM] * 2, flops, nbytes,
    )(place, row_ids, live_count, tiles, held)
    total = call(
        functools.partial(tile_sums, masks_even, masks_odd, True, True),
        jax.ShapeDtypeStruct((n_rep * rows, width), BF16 if n_rep == 2 else F32),
        [SMEM] * 3 + [VMEM] * 3, flops, nbytes,
    )(place, row_ids, live_count, tiles, other_held, own)

    for bit in rep_bits[:-1]:
        half = bit * rows
        got = swap(total[half:].astype(BF16), n_node, n_rep, (0, bit), (0, bit))
        total = total[:half].astype(F32) + got.astype(F32)
    total = total.astype(BF16)
    got = swap(total, n_node, n_rep, (0, 1), (0, 1))

    grad_shape = jax.ShapeDtypeStruct((width, width), F32)
    layer_out, keep, send = call(
        update,
        (jax.ShapeDtypeStruct((rows, width), BF16), grad_shape, grad_shape),
        [SMEM] + [VMEM] * 8, 16 * rows * width * width, 1 << 20,
    )(place, total, got, feats, far[:rows], out_grad, far[rows:], w_self, w_neigh)
    grad = keep + swap(send, n_node, n_rep, (1, 0), (1, 0))

    order_even = chip_bits[::-1]
    order_odd = chip_bits[:1] + order_even[:-1]
    steps = [((0, bit), (0, bit)) for bit in rep_bits[:-1]]
    steps += [((even, 0), (odd, 0)) for even, odd in zip(order_even, order_odd, strict=True)]
    for even, odd in steps:
        part = grad.astype(BF16)
        grad = part.astype(F32) + swap(part, n_node, n_rep, even, odd).astype(F32)
    other_grad = swap(grad, n_node, n_rep, (1, 0), (1, 0))
    first_core = (place[0] & 1) == 0
    grad_self = jnp.where(first_core, grad, other_grad)
    grad_neigh = jnp.where(first_core, other_grad, grad)
    return (layer_out, grad_self, grad_neigh)


def solution(mesh):
    placed = (
        P(("node", "rep"), None),
        P("node", "rep", None, None, None, None),
        P("node", "rep", None, None),
        P("node", "rep", None),
        P(),
        P(),
        P(("node", "rep"), None),
    )
    return jax.shard_map(
        functools.partial(local, mesh.shape["node"], mesh.shape["rep"]),
        mesh=mesh,
        in_specs=placed,
        out_specs=(P(("node", "rep"), None), P(), P()),
        check_vma=False,
    )
```

```python
import functools

import jax
import jax.numpy as jnp
from jax import lax
from jax.experimental import pallas as pl
from jax.experimental.pallas import tpu as pltpu
from jax.sharding import PartitionSpec as P

VMEM = pl.BlockSpec(memory_space=pltpu.VMEM)
SMEM = pl.BlockSpec(memory_space=pltpu.SMEM)
F32 = jnp.float32
BF16 = jnp.bfloat16


def bits_below(size):
    return [1 << i for i in reversed(range(size.bit_length() - 1))]


def doubling_masks(bits):
    masks = [0]
    for bit in bits:
        masks = masks + [mask ^ bit for mask in masks]
    return masks


def swap(x, n_node, n_rep, even, odd):
    pairs = []
    for node in range(n_node):
        flip_node, flip_rep = odd if node.bit_count() & 1 else even
        for rep in range(n_rep):
            pairs.append((node * n_rep + rep, (node ^ flip_node) * n_rep + (rep ^ flip_rep)))
    return lax.ppermute(x, ("node", "rep"), pairs)


def masked_pair(place, rows, count, tiles, out_tiles, mates, even, odd):
    node = place[0]
    base = place[1] - place[3]
    groups = []
    for mate, e, o in zip(mates, even, odd, strict=True):
        origin = node ^ 1 if mate else node
        groups.append(origin ^ jnp.where(place[2] == (0 if mate else 1), o, e))
    lefts = []
    for s in range(tiles.shape[1]):
        for k in range(out_tiles):
            parts = []
            for group in groups:
                live = jnp.logical_and(s < count[group], rows[group * tiles.shape[1] + s] == base ^ k)
                value = tiles[group, s]
                chosen = jnp.full(value.shape, live.astype(F32)) > 0.5
                parts.append(jnp.where(chosen, value, jnp.zeros_like(value)))
            lefts.append(jnp.concatenate(parts, axis=1))
    return jnp.concatenate(lefts, axis=0)


def build_lefts(steps, place, rows, count, tiles, *outs):
    at = 0
    for out in outs:
        for i in range(out.shape[0]):
            out_tiles = out.shape[1] // (tiles.shape[1] * tiles.shape[2])
            out[i] = masked_pair(place, rows, count, tiles, out_tiles, *steps[at])
            at += 1


def tile_sums(steps, prebuilt, n_columns, seeded, *refs):
    refs, out = refs[:-1], refs[-1]
    if seeded:
        refs, seed = refs[:-1], refs[-1]
    refs, columns = refs[:-n_columns], refs[-n_columns:]
    total = seed[...] if seeded else None
    panel = out.shape[0]
    tile = sum(part.shape[0] for part in columns) // (2 * len(steps))
    at = 0
    for part in columns:
        for i in range(0, part.shape[0], 2 * tile):
            size = 2 * tile
            if prebuilt:
                left = refs[0][at]
            else:
                left = masked_pair(*refs, panel // refs[3].shape[2], *steps[at])
            terms = jnp.dot(left, part[i : i + size, :], preferred_element_type=F32)
            for s in range(terms.shape[0] // panel):
                term = terms[s * panel : (s + 1) * panel]
                total = term if total is None else total + term
            at += 1
    out[...] = total.astype(out.dtype)


def update(place, own, got, feats, far_feats, out_grad, far_out_grad, w_self, w_neigh, value, keep_top, keep_low, send_top, send_low, side):
    side[...] = jnp.full(side.shape, place[2])
    rows = feats.shape[0]
    first_rep = jnp.full((rows, feats.shape[1]), place[3]) == 0

    def in_order(mine, far):
        return jnp.concatenate([jnp.where(first_rep, mine, far), jnp.where(first_rep, far, mine)], axis=0)

    x = in_order(feats[...], far_feats[...])
    g = in_order(out_grad[...], far_out_grad[...]).astype(F32)
    aggregate = (own[...].astype(F32) + got[...].astype(F32)).astype(BF16)
    pre = jnp.dot(x, w_self[...], preferred_element_type=F32) + jnp.dot(
        aggregate, w_neigh[...], preferred_element_type=F32
    )
    sigma = jax.nn.sigmoid(pre)
    both = (pre * sigma).astype(BF16)
    value[...] = jnp.where(first_rep, both[:rows], both[rows:])
    delta = (g * sigma * (1.0 + pre * (1.0 - sigma))).astype(BF16)
    first_core = jnp.full(x.shape, place[2]) == 0
    for left, top, low in (
        (jnp.where(first_core, aggregate, x), send_top, send_low),
        (jnp.where(first_core, x, aggregate), keep_top, keep_low),
    ):
        grad = lax.dot_general(left, delta, (((0,), (0,)), ((), ())), preferred_element_type=F32)
        top[...] = grad[: top.shape[0]]
        low[...] = grad[top.shape[0] :]


def copied(x_ref, out_ref):
    out_ref[...] = x_ref[...]


def call(body, out_shape, specs, flops, nbytes):
    return pl.pallas_call(
        body,
        out_shape=out_shape,
        in_specs=specs,
        out_specs=jax.tree.map(lambda _: VMEM, out_shape),
        cost_estimate=pl.CostEstimate(flops=flops, bytes_accessed=nbytes, transcendentals=0),
        compiler_params=pltpu.CompilerParams(vmem_limit_bytes=24 * 1024 * 1024),
    )


def local(n_node, n_rep, node_feats, tile_vals, tile_rows, tile_count, w_self, w_neigh, out_grad):
    tiles = tile_vals[0, 0]
    rows, width = node_feats.shape
    node, rep = lax.axis_index("node"), lax.axis_index("rep")
    barrier = lax.optimization_barrier

    hops = [bit | 1 for bit in bits_below(n_node)[:-1]]
    turned = hops[-1:] + hops[:-1]
    rep_bits = bits_below(n_rep)

    def trade(x, even, odd):
        return swap(x, n_node, n_rep, even, odd)

    def core_swap(x):
        return trade(x, (1, 0), (1, 0))

    got = trade(node_feats, (hops[0], 0), (turned[0], 0))
    feats = call(copied, jax.ShapeDtypeStruct(node_feats.shape, BF16), [VMEM], 0, node_feats.size * 4)(node_feats)
    far = trade(jnp.concatenate([feats, out_grad], axis=0), (0, 1), (0, 1))
    feats, got, tables = barrier((feats, got, (node, rep, tile_rows, tile_count)))
    node, rep, tile_rows, tile_count = tables
    row_ids = tile_rows[0, 0].reshape(-1)
    live_count = tile_count[0, 0]
    parity = node
    for shift in bits_below(n_node.bit_length()):
        parity = parity ^ (parity >> shift)
    place = jnp.stack([node, rep, parity & 1, rep & 1]).astype(jnp.int32)
    held = jnp.concatenate([feats, got], axis=0)
    for even, odd in zip(hops[1:-1], turned[1:-1], strict=True):
        got = trade(held, (even, 0), (odd, 0))
        far, got, place, row_ids, live_count = barrier((far, got, place, row_ids, live_count))
        held = jnp.concatenate([held, got], axis=0)
    late = trade(held, (hops[-1], 0), (turned[-1], 0))
    other = core_swap(held)

    masks_even, masks_odd = doubling_masks(hops), doubling_masks(turned)
    half = len(masks_even) // 2

    def steps_of(mate, first):
        return [
            ((mate, mate), masks_even[i : i + 2], masks_odd[i : i + 2]) for i in range(first, first + half, 2)
        ]

    groups = [steps_of(False, 0), steps_of(False, half), steps_of(True, 0) + steps_of(True, half)]
    panel = n_rep * rows
    slots = tiles.shape[1]
    left_sizes = [len(steps) * slots * panel * 2 * rows * 2 for steps in groups]
    prebuilt = sum(left_sizes) <= 4 * 1024 * 1024
    tables = [place, row_ids, live_count, tiles]
    table_specs = [SMEM] * 3 + [VMEM]
    if prebuilt:
        lefts = call(
            functools.partial(build_lefts, sum(groups, [])),
            tuple(jax.ShapeDtypeStruct((len(steps), slots * panel, 2 * rows), BF16) for steps in groups),
            table_specs, 0, 3 * sum(left_sizes),
        )(*tables)

    def sums(index, columns, seed, dtype):
        steps = groups[index]
        given, specs = ([lefts[index]], [VMEM]) if prebuilt else (tables, table_specs)
        more = columns + ([seed] if seed is not None else [])
        flops = len(steps) * slots * panel * 2 * rows * width * 2
        return call(
            functools.partial(tile_sums, steps, prebuilt, len(columns), seed is not None),
            jax.ShapeDtypeStruct((panel, width), dtype), specs + [VMEM] * len(more), flops, left_sizes[index],
        )(*given, *more)

    total = sums(0, [held], None, F32)
    late, total = barrier((late, total))
    other_late = core_swap(late)
    total = sums(1, [late], total, F32)
    total = sums(2, [other, other_late], total, BF16 if n_rep == 2 else F32)

    for bit in rep_bits[:-1]:
        got = trade(total[bit * rows :].astype(BF16), (0, bit), (0, bit))
        total = total[: bit * rows].astype(F32) + got.astype(F32)
    total = total.astype(BF16)
    got = trade(total, (0, 1), (0, 1))

    half_grad = jax.ShapeDtypeStruct((width // 2, width), F32)
    value, keep_top, keep_low, send_top, send_low, side = call(
        update,
        (
            jax.ShapeDtypeStruct((rows, width), BF16), half_grad, half_grad, half_grad, half_grad,
            jax.ShapeDtypeStruct((1, width), jnp.int32),
        ),
        [SMEM] + [VMEM] * 8, 16 * rows * width * width, 1 << 20,
    )(place, total, got, feats, far[:rows], out_grad, far[rows:], w_self, w_neigh)
    grads = [keep_top + core_swap(send_top), keep_low + core_swap(send_low)]
    layer_out = call(copied, jax.ShapeDtypeStruct((rows, width), BF16), [VMEM], 0, 4 * rows * width)(value)

    order_even = hops
    order_odd = hops[::-1]
    steps = [((0, bit), (0, bit)) for bit in rep_bits[:-1]]
    steps += [((even, 0), (odd, 0)) for even, odd in zip(order_even, order_odd, strict=True)]
    for even, odd in steps[:-1]:
        parts = [grad.astype(BF16) for grad in grads]
        gots = [trade(part, even, odd) for part in parts]
        gots[0], layer_out = barrier((gots[0], layer_out))
        grads = [part.astype(F32) + got.astype(F32) for part, got in zip(parts, gots, strict=True)]
    parts = [grad.astype(BF16) for grad in grads]
    gots = [trade(part, *steps[-1]) for part in parts]
    part, got = jnp.concatenate(parts, axis=0), jnp.concatenate(gots, axis=0)
    other_part = core_swap(part)
    other_got = jnp.concatenate([core_swap(got) for got in gots], axis=0)
    grad = part.astype(F32) + got.astype(F32)
    other_grad = other_part.astype(F32) + other_got.astype(F32)
    first_core = side == 0
    grad_self = jnp.where(first_core, grad, other_grad)
    grad_neigh = jnp.where(first_core, other_grad, grad)
    return (layer_out, grad_self, grad_neigh)


def solution(mesh):
    placed = (
        P(("node", "rep"), None),
        P("node", "rep", None, None, None, None),
        P("node", "rep", None, None),
        P("node", "rep", None),
        P(),
        P(),
        P(("node", "rep"), None),
    )
    return jax.shard_map(
        functools.partial(local, mesh.shape["node"], mesh.shape["rep"]),
        mesh=mesh,
        in_specs=placed,
        out_specs=(P(("node", "rep"), None), P(), P()),
        check_vma=False,
    )
```

```python
import functools

import jax
import jax.numpy as jnp
from jax import lax
from jax.experimental import pallas as pl
from jax.experimental.pallas import tpu as pltpu
from jax.sharding import PartitionSpec as P

VMEM = pl.BlockSpec(memory_space=pltpu.VMEM)
SMEM = pl.BlockSpec(memory_space=pltpu.SMEM)
F32 = jnp.float32
BF16 = jnp.bfloat16


def bits_below(size):
    return [1 << i for i in reversed(range(size.bit_length() - 1))]


def doubling_masks(bits):
    masks = [0]
    for bit in bits:
        masks = masks + [mask ^ bit for mask in masks]
    return masks


def swap(x, n_node, n_rep, even, odd):
    pairs = []
    for node in range(n_node):
        flip_node, flip_rep = odd if node.bit_count() & 1 else even
        for rep in range(n_rep):
            pairs.append((node * n_rep + rep, (node ^ flip_node) * n_rep + (rep ^ flip_rep)))
    return lax.ppermute(x, ("node", "rep"), pairs)


def masked_pair(place, rows, count, tiles, out_tiles, mates, even, odd):
    node = place[0]
    base = place[1] - place[3]
    groups = []
    for mate, e, o in zip(mates, even, odd, strict=True):
        origin = node ^ 1 if mate else node
        groups.append(origin ^ jnp.where(place[2] == (0 if mate else 1), o, e))
    lefts = []
    for s in range(tiles.shape[1]):
        for k in range(out_tiles):
            parts = []
            for group in groups:
                live = jnp.logical_and(s < count[group], rows[group * tiles.shape[1] + s] == base ^ k)
                value = tiles[group, s]
                chosen = jnp.full(value.shape, live.astype(F32)) > 0.5
                parts.append(jnp.where(chosen, value, jnp.zeros_like(value)))
            lefts.append(jnp.concatenate(parts, axis=1))
    return jnp.concatenate(lefts, axis=0)


def build_lefts(steps, place, rows, count, tiles, *outs):
    at = 0
    for out in outs:
        for i in range(out.shape[0]):
            out_tiles = out.shape[1] // (tiles.shape[1] * tiles.shape[2])
            out[i] = masked_pair(place, rows, count, tiles, out_tiles, *steps[at])
            at += 1


def tile_sums(groups, prebuilt, n_columns, seeded, *refs):
    refs, out = refs[:-1], refs[-1]
    if seeded:
        refs, seed = refs[:-1], refs[-1]
    refs, columns = refs[:-n_columns], refs[-n_columns:]
    total = seed[...] if seeded else None
    panel = out.shape[0]
    size = sum(part.shape[0] for part in columns) // sum(len(steps) for steps in groups)
    blocks = [part.at[pl.ds(i, size), :] for part in columns for i in range(0, part.shape[0], size)]
    for at, steps in enumerate(groups):
        for i, step in enumerate(steps):
            if prebuilt:
                left = refs[at][i]
            else:
                left = masked_pair(*refs, panel // refs[3].shape[2], *step)
            terms = jnp.dot(left, blocks.pop(0)[...], preferred_element_type=F32)
            for s in range(terms.shape[0] // panel):
                term = terms[s * panel : (s + 1) * panel]
                total = term if total is None else total + term
    out[...] = total.astype(out.dtype)


def summed(total, got):
    return (total[...].astype(F32) + got[...].astype(F32)).astype(BF16)


def in_order(place, mine, far):
    first_rep = jnp.full(mine.shape, place[3]) == 0
    return jnp.concatenate(
        [jnp.where(first_rep, mine[...], far[...]), jnp.where(first_rep, far[...], mine[...])], axis=0
    )


def update_first(place, total, got, feats, far_feats, w_self, w_neigh, x, aggregate, pre):
    x[...] = in_order(place, feats, far_feats)
    aggregate[...] = summed(total, got)
    pre[...] = jnp.dot(x[...], w_self[...], preferred_element_type=F32) + jnp.dot(
        aggregate[...], w_neigh[: aggregate.shape[1], :], preferred_element_type=F32
    )


def update_second(place, total, got, x, first_aggregate, first_pre, out_grad, far_out_grad, w_neigh, *outs):
    value, keep_top, keep_low, send_top, send_low, side = outs
    side[...] = jnp.full(side.shape, place[2])
    rows, split = out_grad.shape[0], first_aggregate.shape[1]
    second_aggregate = summed(total, got)
    aggregate = jnp.concatenate([first_aggregate[...], second_aggregate], axis=1)
    pre = first_pre[...] + jnp.dot(second_aggregate, w_neigh[split:, :], preferred_element_type=F32)
    sigma = jax.nn.sigmoid(pre)
    both = (pre * sigma).astype(BF16)
    value[...] = jnp.where(jnp.full(value.shape, place[3]) == 0, both[:rows], both[rows:])
    g = in_order(place, out_grad, far_out_grad).astype(F32)
    delta = (g * sigma * (1.0 + pre * (1.0 - sigma))).astype(BF16)
    first_core = jnp.full(x.shape, place[2]) == 0
    for left, top, low in (
        (jnp.where(first_core, aggregate, x[...]), send_top, send_low),
        (jnp.where(first_core, x[...], aggregate), keep_top, keep_low),
    ):
        grad = lax.dot_general(left, delta, (((0,), (0,)), ((), ())), preferred_element_type=F32)
        top[...] = grad[: top.shape[0]]
        low[...] = grad[top.shape[0] :]


def copied(x_ref, out_ref):
    out_ref[...] = x_ref[...]


def call(body, out_shape, specs, flops, nbytes):
    return pl.pallas_call(
        body,
        out_shape=out_shape,
        in_specs=specs,
        out_specs=jax.tree.map(lambda _: VMEM, out_shape),
        cost_estimate=pl.CostEstimate(flops=flops, bytes_accessed=nbytes, transcendentals=0),
        compiler_params=pltpu.CompilerParams(vmem_limit_bytes=24 * 1024 * 1024),
    )


def local(n_node, n_rep, node_feats, tile_vals, tile_rows, tile_count, w_self, w_neigh, out_grad):
    tiles = tile_vals[0, 0]
    rows, width = node_feats.shape
    node, rep = lax.axis_index("node"), lax.axis_index("rep")
    barrier = lax.optimization_barrier

    hops = [bit | 1 for bit in bits_below(n_node)[:-1]]
    plain = hops
    hops, turned = [plain[1], plain[0], plain[2]], [plain[0], plain[2], plain[1]]
    rep_bits = bits_below(n_rep)

    def trade(x, even, odd):
        return swap(x, n_node, n_rep, even, odd)

    def core_swap(x):
        return trade(x, (1, 0), (1, 0))

    got = trade(node_feats, (hops[0], 0), (turned[0], 0))
    feats = call(copied, jax.ShapeDtypeStruct(node_feats.shape, BF16), [VMEM], 0, node_feats.size * 4)(node_feats)
    far = trade(jnp.concatenate([feats, out_grad], axis=0), (0, 1), (0, 1))
    feats, got, tables = barrier((feats, got, (node, rep, tile_rows, tile_count)))
    node, rep, tile_rows, tile_count = tables
    row_ids = tile_rows[0, 0].reshape(-1)
    live_count = tile_count[0, 0]
    parity = node
    for shift in bits_below(n_node.bit_length()):
        parity = parity ^ (parity >> shift)
    place = jnp.stack([node, rep, parity & 1, rep & 1]).astype(jnp.int32)
    masks_even, masks_odd = doubling_masks(hops), doubling_masks(turned)
    pairs = [
        [((mate, mate), masks_even[i : i + 2], masks_odd[i : i + 2]) for i in range(0, len(masks_even), 2)]
        for mate in (False, True)
    ]
    early = len(pairs[0]) // 2
    groups = [pairs[0][:early], pairs[0][early:], pairs[1]]
    panel = n_rep * rows
    slots = tiles.shape[1]
    left_sizes = [len(steps) * slots * panel * 2 * rows * 2 for steps in groups]
    prebuilt = sum(left_sizes) <= 4 * 1024 * 1024
    halves = [slice(0, width // 2), slice(width // 2, width)]
    held = [jnp.concatenate([feats[:, half], got[:, half]], axis=0) for half in halves]
    for even, odd in zip(hops[1:-1], turned[1:-1], strict=True):
        gots = [trade(part, (even, 0), (odd, 0)) for part in held]
        gots[0], place, row_ids, live_count = barrier((gots[0], place, row_ids, live_count))
        gots[-1], far = barrier((gots[-1], far))
        held = [jnp.concatenate([part, got], axis=0) for part, got in zip(held, gots, strict=True)]
    tables = [place, row_ids, live_count, tiles]
    table_specs = [SMEM] * 3 + [VMEM]
    gots = [trade(part, (hops[-1], 0), (turned[-1], 0)) for part in held]
    if prebuilt:
        lefts = call(
            functools.partial(build_lefts, sum(groups, [])),
            tuple(jax.ShapeDtypeStruct((len(steps), slots * panel, 2 * rows), BF16) for steps in groups),
            table_specs, 0, 3 * sum(left_sizes),
        )(*tables)
        gots[0], lefts = barrier((gots[0], lefts))

    def sums(indices, columns, seed, dtype):
        steps = [groups[i] for i in indices]
        given, specs = ([lefts[i] for i in indices], [VMEM] * len(indices)) if prebuilt else (tables, table_specs)
        more = columns + ([seed] if seed is not None else [])
        size = sum(left_sizes[i] for i in indices)
        return call(
            functools.partial(tile_sums, steps, prebuilt, len(columns), seed is not None),
            jax.ShapeDtypeStruct((panel, columns[0].shape[1]), dtype),
            specs + [VMEM] * len(more), size * columns[0].shape[1], size,
        )(*given, *more)

    sums_type = BF16 if n_rep == 2 else F32
    first = jnp.concatenate([held[0], gots[0]], axis=0)
    own = sums([0, 1], [first], None, F32)
    gots[1], own = barrier((gots[1], own))
    second = jnp.concatenate([held[1], gots[1]], axis=0)
    total = sums([2], [core_swap(first)], own, sums_type)
    mates = core_swap(second)
    second, total = barrier((second, total))
    totals = [total, sums([0, 1, 2], [second, mates], None, sums_type)]

    gots = []
    for i in (0, 1):
        for bit in rep_bits[:-1]:
            got = trade(totals[i][bit * rows :].astype(BF16), (0, bit), (0, bit))
            totals[i] = totals[i][: bit * rows].astype(F32) + got.astype(F32)
        totals[i] = totals[i].astype(BF16)
        gots.append(trade(totals[i], (0, 1), (0, 1)))

    two_blocks = (2 * rows, width)
    x, aggregate, pre = call(
        update_first,
        (
            jax.ShapeDtypeStruct(two_blocks, BF16),
            jax.ShapeDtypeStruct(totals[0].shape, BF16),
            jax.ShapeDtypeStruct(two_blocks, F32),
        ),
        [SMEM] + [VMEM] * 6, 6 * rows * width * width, 1 << 19,
    )(place, totals[0], gots[0], feats, far[:rows], w_self, w_neigh)
    half_grad = jax.ShapeDtypeStruct((width // 2, width), F32)
    value, keep_top, keep_low, send_top, send_low, side = call(
        update_second,
        (
            jax.ShapeDtypeStruct((rows, width), BF16), half_grad, half_grad, half_grad, half_grad,
            jax.ShapeDtypeStruct((1, width), jnp.int32),
        ),
        [SMEM] + [VMEM] * 8, 10 * rows * width * width, 1 << 20,
    )(place, totals[1], gots[1], x, aggregate, pre, out_grad, far[rows:], w_neigh)
    grads = [keep_top + core_swap(send_top), keep_low + core_swap(send_low)]
    layer_out = call(copied, jax.ShapeDtypeStruct((rows, width), BF16), [VMEM], 0, 4 * rows * width)(value)

    order_even = [plain[0], plain[2], plain[1]]
    order_odd = [plain[1], plain[0], plain[2]]
    steps = [((0, bit), (0, bit)) for bit in rep_bits[:-1]]
    steps += [((even, 0), (odd, 0)) for even, odd in zip(order_even, order_odd, strict=True)]
    for even, odd in steps[:-1]:
        parts = [grad.astype(BF16) for grad in grads]
        gots = [trade(part, even, odd) for part in parts]
        gots[0], layer_out = barrier((gots[0], layer_out))
        grads = [part.astype(F32) + got.astype(F32) for part, got in zip(parts, gots, strict=True)]
    parts = [grad.astype(BF16) for grad in grads]
    gots = [trade(part, *steps[-1]) for part in parts]
    part, got = jnp.concatenate(parts, axis=0), jnp.concatenate(gots, axis=0)
    other_part = core_swap(part)
    other_got = jnp.concatenate([core_swap(got) for got in gots], axis=0)
    grad = part.astype(F32) + got.astype(F32)
    other_grad = other_part.astype(F32) + other_got.astype(F32)
    first_core = side == 0
    grad_self = jnp.where(first_core, grad, other_grad)
    grad_neigh = jnp.where(first_core, other_grad, grad)
    return (layer_out, grad_self, grad_neigh)


def solution(mesh):
    placed = (
        P(("node", "rep"), None),
        P("node", "rep", None, None, None, None),
        P("node", "rep", None, None),
        P("node", "rep", None),
        P(),
        P(),
        P(("node", "rep"), None),
    )
    return jax.shard_map(
        functools.partial(local, mesh.shape["node"], mesh.shape["rep"]),
        mesh=mesh,
        in_specs=placed,
        out_specs=(P(("node", "rep"), None), P(), P()),
        check_vma=False,
    )
```

```python
import functools

import jax
import jax.numpy as jnp
from jax import lax
from jax.experimental import pallas as pl
from jax.experimental.pallas import tpu as pltpu
from jax.sharding import PartitionSpec as P

VMEM = pl.BlockSpec(memory_space=pltpu.VMEM)
SMEM = pl.BlockSpec(memory_space=pltpu.SMEM)
F32 = jnp.float32
BF16 = jnp.bfloat16


def bits_below(size):
    return [1 << i for i in reversed(range(size.bit_length() - 1))]


def doubling_masks(bits):
    masks = [0]
    for bit in bits:
        masks = masks + [mask ^ bit for mask in masks]
    return masks


def swap(x, n_node, n_rep, even, odd):
    pairs = []
    for node in range(n_node):
        flip_node, flip_rep = odd if node.bit_count() & 1 else even
        for rep in range(n_rep):
            pairs.append((node * n_rep + rep, (node ^ flip_node) * n_rep + (rep ^ flip_rep)))
    return lax.ppermute(x, ("node", "rep"), pairs)


def masked_pair(place, rows, count, tiles, out_tiles, mates, even, odd):
    node = place[0]
    base = place[1] - place[3]
    groups = []
    for mate, e, o in zip(mates, even, odd, strict=True):
        origin = node ^ 1 if mate else node
        groups.append(origin ^ jnp.where(place[2] == (0 if mate else 1), o, e))
    lefts = []
    for s in range(tiles.shape[1]):
        for k in range(out_tiles):
            parts = []
            for group in groups:
                live = jnp.logical_and(s < count[group], rows[group * tiles.shape[1] + s] == base ^ k)
                value = tiles[group, s]
                chosen = jnp.full(value.shape, live.astype(F32)) > 0.5
                parts.append(jnp.where(chosen, value, jnp.zeros_like(value)))
            lefts.append(jnp.concatenate(parts, axis=1))
    return jnp.concatenate(lefts, axis=0)


def build_lefts(steps, place, rows, count, tiles, *outs):
    at = 0
    for out in outs:
        for i in range(out.shape[0]):
            out_tiles = out.shape[1] // (tiles.shape[1] * tiles.shape[2])
            out[i] = masked_pair(place, rows, count, tiles, out_tiles, *steps[at])
            at += 1


def tile_sums(groups, prebuilt, n_columns, seeded, *refs):
    refs, out = refs[:-1], refs[-1]
    if seeded:
        refs, seed = refs[:-1], refs[-1]
    refs, columns = refs[:-n_columns], refs[-n_columns:]
    total = seed[...] if seeded else None
    panel = out.shape[0]
    size = sum(part.shape[0] for part in columns) // sum(len(steps) for steps in groups)
    blocks = [part.at[pl.ds(i, size), :] for part in columns for i in range(0, part.shape[0], size)]
    for at, steps in enumerate(groups):
        for i, step in enumerate(steps):
            if prebuilt:
                left = refs[at][i]
            else:
                left = masked_pair(*refs, panel // refs[3].shape[2], *step)
            terms = jnp.dot(left, blocks.pop(0)[...], preferred_element_type=F32)
            for s in range(terms.shape[0] // panel):
                term = terms[s * panel : (s + 1) * panel]
                total = term if total is None else total + term
    out[...] = total.astype(out.dtype)


def summed(total, got):
    return (total[...].astype(F32) + got[...].astype(F32)).astype(BF16)


def flag_like(flags, i, x):
    return jnp.broadcast_to(flags[i : i + 1, : x.shape[1]], x.shape) == 0


def in_order(flags, mine, far):
    first_rep = flag_like(flags, 1, mine)
    return jnp.concatenate(
        [jnp.where(first_rep, mine[...], far[...]), jnp.where(first_rep, far[...], mine[...])], axis=0
    )


def update_first(flags, total, got, feats, far_feats, w_self, w_neigh, x, aggregate, pre):
    x[...] = in_order(flags, feats, far_feats)
    aggregate[...] = summed(total, got)
    pre[...] = jnp.dot(x[...], w_self[...], preferred_element_type=F32) + jnp.dot(
        aggregate[...], w_neigh[: aggregate.shape[1], :], preferred_element_type=F32
    )


def update_second(flags, total, got, x, first_aggregate, first_pre, out_grad, far_out_grad, w_neigh, *outs):
    value, keep_top, keep_low, send_top, send_low = outs
    rows, split = out_grad.shape[0], first_aggregate.shape[1]
    second_aggregate = summed(total, got)
    aggregate = jnp.concatenate([first_aggregate[...], second_aggregate], axis=1)
    pre = first_pre[...] + jnp.dot(second_aggregate, w_neigh[split:, :], preferred_element_type=F32)
    sigma = jax.nn.sigmoid(pre)
    both = (pre * sigma).astype(BF16)
    value[...] = jnp.where(flag_like(flags, 1, value), both[:rows], both[rows:])
    g = in_order(flags, out_grad, far_out_grad).astype(F32)
    delta = (g * sigma * (1.0 + pre * (1.0 - sigma))).astype(BF16)
    first_core = flag_like(flags, 0, x)
    for left, top, low in (
        (jnp.where(first_core, aggregate, x[...]), send_top, send_low),
        (jnp.where(first_core, x[...], aggregate), keep_top, keep_low),
    ):
        grad = lax.dot_general(left, delta, (((0,), (0,)), ((), ())), preferred_element_type=F32)
        top[...] = grad[: top.shape[0]]
        low[...] = grad[top.shape[0] :]


def copied(x_ref, out_ref):
    out_ref[...] = x_ref[...]


def call(body, out_shape, specs, flops, nbytes):
    return pl.pallas_call(
        body,
        out_shape=out_shape,
        in_specs=specs,
        out_specs=jax.tree.map(lambda _: VMEM, out_shape),
        cost_estimate=pl.CostEstimate(flops=flops, bytes_accessed=nbytes, transcendentals=0),
        compiler_params=pltpu.CompilerParams(vmem_limit_bytes=24 * 1024 * 1024),
    )


def local(n_node, n_rep, node_feats, tile_vals, tile_rows, tile_count, w_self, w_neigh, out_grad):
    tiles = tile_vals[0, 0]
    rows, width = node_feats.shape
    node, rep = lax.axis_index("node"), lax.axis_index("rep")
    barrier = lax.optimization_barrier

    bits = [bit | 1 for bit in bits_below(n_node)[:-1]]
    hops, turned = bits[1:2] + bits[:1] + bits[2:], bits[:1] + bits[2:] + bits[1:2]
    rep_bits = bits_below(n_rep)

    def trade(x, even, odd):
        return swap(x, n_node, n_rep, even, odd)

    def core_swap(x):
        return trade(x, (1, 0), (1, 0))

    got = trade(node_feats, (hops[0], 0), (turned[0], 0))
    feats = call(copied, jax.ShapeDtypeStruct(node_feats.shape, BF16), [VMEM], 0, node_feats.size * 4)(node_feats)
    far = trade(jnp.concatenate([feats, out_grad], axis=0), (0, 1), (0, 1))
    feats, got, tables = barrier((feats, got, (node, rep, tile_rows, tile_count)))
    node, rep, tile_rows, tile_count = tables
    row_ids = tile_rows[0, 0].reshape(-1)
    live_count = tile_count[0, 0]
    parity = node
    for shift in reversed(range((n_node.bit_length() - 2).bit_length())):
        parity = parity ^ (parity >> (1 << shift))
    place = jnp.stack([node, rep, parity & 1, rep & 1]).astype(jnp.int32)
    flags = jnp.broadcast_to(place[2:, None], (2, width))
    masks_even, masks_odd = doubling_masks(hops), doubling_masks(turned)
    pairs = [
        [((mate, mate), masks_even[i : i + 2], masks_odd[i : i + 2]) for i in range(0, len(masks_even), 2)]
        for mate in (False, True)
    ]
    early = len(pairs[0]) // 2
    groups = [pairs[0][:early], pairs[0][early:], pairs[1]]
    panel = n_rep * rows
    slots = tiles.shape[1]
    left_sizes = [len(steps) * slots * panel * 2 * rows * 2 for steps in groups]
    prebuilt = sum(left_sizes) <= 4 * 1024 * 1024
    halves = [slice(0, width // 2), slice(width // 2, width)]
    held = [jnp.concatenate([feats[:, half], got[:, half]], axis=0) for half in halves]
    for even, odd in zip(hops[1:-1], turned[1:-1], strict=True):
        gots = [trade(part, (even, 0), (odd, 0)) for part in held]
        gots[0], place, flags, row_ids, live_count = barrier((gots[0], place, flags, row_ids, live_count))
        gots[-1], far = barrier((gots[-1], far))
        held = [jnp.concatenate([part, got], axis=0) for part, got in zip(held, gots, strict=True)]
    tables = [place, row_ids, live_count, tiles]
    table_specs = [SMEM] * 3 + [VMEM]
    gots = [trade(part, (hops[-1], 0), (turned[-1], 0)) for part in held]
    if prebuilt:
        lefts = call(
            functools.partial(build_lefts, sum(groups, [])),
            tuple(jax.ShapeDtypeStruct((len(steps), slots * panel, 2 * rows), BF16) for steps in groups),
            table_specs, 0, 3 * sum(left_sizes),
        )(*tables)
        gots[0], lefts = barrier((gots[0], lefts))

    def sums(indices, columns, seed, dtype):
        steps = [groups[i] for i in indices]
        given, specs = ([lefts[i] for i in indices], [VMEM] * len(indices)) if prebuilt else (tables, table_specs)
        more = columns + ([seed] if seed is not None else [])
        size = sum(left_sizes[i] for i in indices)
        return call(
            functools.partial(tile_sums, steps, prebuilt, len(columns), seed is not None),
            jax.ShapeDtypeStruct((panel, columns[0].shape[1]), dtype),
            specs + [VMEM] * len(more), size * columns[0].shape[1], size,
        )(*given, *more)

    sums_type = BF16 if n_rep == 2 else F32
    first = jnp.concatenate([held[0], gots[0]], axis=0)
    own = sums([0, 1], [first], None, F32)
    gots[1], own = barrier((gots[1], own))
    second = jnp.concatenate([held[1], gots[1]], axis=0)
    total = sums([2], [core_swap(first)], own, sums_type)
    mates = core_swap(second)
    second, total = barrier((second, total))
    totals = [total, sums([0, 1, 2], [second, mates], None, sums_type)]

    gots = []
    for i in (0, 1):
        for bit in rep_bits[:-1]:
            got = trade(totals[i][bit * rows :].astype(BF16), (0, bit), (0, bit))
            totals[i] = totals[i][: bit * rows].astype(F32) + got.astype(F32)
        totals[i] = totals[i].astype(BF16)
        gots.append(trade(totals[i], (0, 1), (0, 1)))

    two_blocks = (2 * rows, width)
    x, aggregate, pre = call(
        update_first,
        (
            jax.ShapeDtypeStruct(two_blocks, BF16),
            jax.ShapeDtypeStruct(totals[0].shape, BF16),
            jax.ShapeDtypeStruct(two_blocks, F32),
        ),
        [VMEM] * 7, 6 * rows * width * width, 1 << 19,
    )(flags, totals[0], gots[0], feats, far[:rows], w_self, w_neigh)
    half_grad = jax.ShapeDtypeStruct((width // 2, width), F32)
    value, keep_top, keep_low, send_top, send_low = call(
        update_second,
        (
            jax.ShapeDtypeStruct((rows, width), BF16), half_grad, half_grad, half_grad, half_grad,
        ),
        [VMEM] * 9, 10 * rows * width * width, 1 << 20,
    )(flags, totals[1], gots[1], x, aggregate, pre, out_grad, far[rows:], w_neigh)
    grads = [keep_top + core_swap(send_top), keep_low + core_swap(send_low)]
    layer_out = call(copied, jax.ShapeDtypeStruct((rows, width), BF16), [VMEM], 0, 4 * rows * width)(value)

    steps = [((0, bit), (0, bit)) for bit in rep_bits[:-1]]
    steps += [((even, 0), (odd, 0)) for even, odd in zip(turned, hops, strict=True)]
    for even, odd in steps[:-1]:
        parts = [grad.astype(BF16) for grad in grads]
        gots = [trade(part, even, odd) for part in parts]
        gots[0], layer_out = barrier((gots[0], layer_out))
        grads = [part.astype(F32) + got.astype(F32) for part, got in zip(parts, gots, strict=True)]
    parts = [grad.astype(BF16) for grad in grads]
    gots = [trade(part, *steps[-1]) for part in parts]
    part, got = jnp.concatenate(parts, axis=0), jnp.concatenate(gots, axis=0)
    other_part = core_swap(part)
    other_got = jnp.concatenate([core_swap(got) for got in gots], axis=0)
    grad = part.astype(F32) + got.astype(F32)
    other_grad = other_part.astype(F32) + other_got.astype(F32)
    first_core = flags[:1] == 0
    grad_self = jnp.where(first_core, grad, other_grad)
    grad_neigh = jnp.where(first_core, other_grad, grad)
    return (layer_out, grad_self, grad_neigh)


def solution(mesh):
    placed = (
        P(("node", "rep"), None),
        P("node", "rep", None, None, None, None),
        P("node", "rep", None, None),
        P("node", "rep", None),
        P(),
        P(),
        P(("node", "rep"), None),
    )
    return jax.shard_map(
        functools.partial(local, mesh.shape["node"], mesh.shape["rep"]),
        mesh=mesh,
        in_specs=placed,
        out_specs=(P(("node", "rep"), None), P(), P()),
        check_vma=False,
    )
```

```python
import functools

import jax
import jax.numpy as jnp
from jax import lax
from jax.experimental import pallas as pl
from jax.experimental.pallas import tpu as pltpu
from jax.sharding import PartitionSpec as P

VMEM = pl.BlockSpec(memory_space=pltpu.VMEM)
SMEM = pl.BlockSpec(memory_space=pltpu.SMEM)
F32 = jnp.float32
BF16 = jnp.bfloat16


def bits_below(size):
    return [1 << i for i in reversed(range(size.bit_length() - 1))]


def doubling_masks(bits):
    masks = [0]
    for bit in bits:
        masks = masks + [mask ^ bit for mask in masks]
    return masks


def swap(x, n_node, n_rep, even, odd):
    pairs = []
    for node in range(n_node):
        flip_node, flip_rep = odd if node.bit_count() & 1 else even
        for rep in range(n_rep):
            pairs.append((node * n_rep + rep, (node ^ flip_node) * n_rep + (rep ^ flip_rep)))
    return lax.ppermute(x, ("node", "rep"), pairs)


def masked_pair(place, rows, count, tiles, out_tiles, mates, even, odd):
    node = place[0]
    base = place[1] - place[3]
    groups = []
    for mate, e, o in zip(mates, even, odd, strict=True):
        origin = node ^ 1 if mate else node
        groups.append(origin ^ jnp.where(place[2] == (0 if mate else 1), o, e))
    lefts = []
    for s in range(tiles.shape[1]):
        for k in range(out_tiles):
            parts = []
            for group in groups:
                live = jnp.logical_and(s < count[group], rows[group * tiles.shape[1] + s] == base ^ k)
                value = tiles[group, s]
                chosen = jnp.full(value.shape, live.astype(F32)) > 0.5
                parts.append(jnp.where(chosen, value, jnp.zeros_like(value)))
            lefts.append(jnp.concatenate(parts, axis=1))
    return jnp.concatenate(lefts, axis=0)


def build_lefts(steps, place, rows, count, tiles, *outs):
    at = 0
    for out in outs:
        for i in range(out.shape[0]):
            out_tiles = out.shape[1] // (tiles.shape[1] * tiles.shape[2])
            out[i] = masked_pair(place, rows, count, tiles, out_tiles, *steps[at])
            at += 1


def tile_sums(groups, prebuilt, n_columns, seeded, *refs):
    refs, out = refs[:-1], refs[-1]
    if seeded:
        refs, seed = refs[:-1], refs[-1]
    refs, columns = refs[:-n_columns], refs[-n_columns:]
    total = seed[...] if seeded else None
    panel = out.shape[0]
    size = sum(part.shape[0] for part in columns) // sum(len(steps) for steps in groups)
    blocks = [part.at[pl.ds(i, size), :] for part in columns for i in range(0, part.shape[0], size)]
    for at, steps in enumerate(groups):
        for i, step in enumerate(steps):
            if prebuilt:
                left = refs[at][i]
            else:
                left = masked_pair(*refs, panel // refs[3].shape[2], *step)
            terms = jnp.dot(left, blocks.pop(0)[...], preferred_element_type=F32)
            for s in range(terms.shape[0] // panel):
                term = terms[s * panel : (s + 1) * panel]
                total = term if total is None else total + term
    out[...] = total.astype(out.dtype)


def summed(total, got):
    return (total[...].astype(F32) + got[...].astype(F32)).astype(BF16)


def flag_like(flags, i, x):
    return jnp.broadcast_to(flags[i : i + 1, : x.shape[1]], x.shape) == 0


def in_order(flags, mine, far):
    first_rep = flag_like(flags, 1, mine)
    return jnp.concatenate(
        [jnp.where(first_rep, mine[...], far[...]), jnp.where(first_rep, far[...], mine[...])], axis=0
    )


def update_first(flags, total, got, feats, far_feats, w_self, w_neigh, x, aggregate, pre):
    x[...] = in_order(flags, feats, far_feats)
    aggregate[...] = summed(total, got)
    pre[...] = jnp.dot(x[...], w_self[...], preferred_element_type=F32) + jnp.dot(
        aggregate[...], w_neigh[: aggregate.shape[1], :], preferred_element_type=F32
    )


def update_second(flags, total, got, x, first_aggregate, first_pre, out_grad, far_out_grad, w_neigh, *outs):
    value, keep_top, keep_low, send_top, send_low = outs
    rows, split = out_grad.shape[0], first_aggregate.shape[1]
    second_aggregate = summed(total, got)
    aggregate = jnp.concatenate([first_aggregate[...], second_aggregate], axis=1)
    pre = first_pre[...] + jnp.dot(second_aggregate, w_neigh[split:, :], preferred_element_type=F32)
    sigma = jax.nn.sigmoid(pre)
    both = (pre * sigma).astype(BF16)
    value[...] = jnp.where(flag_like(flags, 1, value), both[:rows], both[rows:])
    g = in_order(flags, out_grad, far_out_grad).astype(F32)
    delta = (g * sigma * (1.0 + pre * (1.0 - sigma))).astype(BF16)
    first_core = flag_like(flags, 0, x)
    for left, top, low in (
        (jnp.where(first_core, aggregate, x[...]), send_top, send_low),
        (jnp.where(first_core, x[...], aggregate), keep_top, keep_low),
    ):
        grad = lax.dot_general(left, delta, (((0,), (0,)), ((), ())), preferred_element_type=F32)
        top[...] = grad[: top.shape[0]]
        low[...] = grad[top.shape[0] :]


def copied(x_ref, out_ref):
    out_ref[...] = x_ref[...]


def call(body, out_shape, specs, flops, nbytes):
    return pl.pallas_call(
        body,
        out_shape=out_shape,
        in_specs=specs,
        out_specs=jax.tree.map(lambda _: VMEM, out_shape),
        cost_estimate=pl.CostEstimate(flops=flops, bytes_accessed=nbytes, transcendentals=0),
        compiler_params=pltpu.CompilerParams(vmem_limit_bytes=24 * 1024 * 1024),
    )


def local(n_node, n_rep, node_feats, tile_vals, tile_rows, tile_count, w_self, w_neigh, out_grad):
    tiles = tile_vals[0, 0]
    rows, width = node_feats.shape
    node, rep = lax.axis_index("node"), lax.axis_index("rep")
    barrier = lax.optimization_barrier

    bits = [bit | 1 for bit in bits_below(n_node)[:-1]]
    hops, turned = bits[:1] + bits[2:] + bits[1:2], bits[1:2] + bits[:1] + bits[2:]
    rep_bits = bits_below(n_rep)

    def trade(x, even, odd):
        return swap(x, n_node, n_rep, even, odd)

    def core_swap(x):
        return trade(x, (1, 0), (1, 0))

    got = trade(node_feats, (hops[0], 0), (turned[0], 0))
    feats = call(copied, jax.ShapeDtypeStruct(node_feats.shape, BF16), [VMEM], 0, node_feats.size * 4)(node_feats)
    far = trade(jnp.concatenate([feats, out_grad], axis=0), (0, 1), (0, 1))
    row_ids = tile_rows[0, 0].reshape(-1)
    feats, got, tables = barrier((feats, got, (node, rep, row_ids, tile_count)))
    node, rep, row_ids, tile_count = tables
    live_count = tile_count[0, 0]
    parity = node
    for shift in reversed(range((n_node.bit_length() - 2).bit_length())):
        parity = parity ^ (parity >> (1 << shift))
    place = jnp.stack([node, rep, parity & 1, rep & 1]).astype(jnp.int32)
    flags = jnp.broadcast_to(place[2:, None], (2, width))
    masks_even, masks_odd = doubling_masks(hops), doubling_masks(turned)
    pairs = [
        [((mate, mate), masks_even[i : i + 2], masks_odd[i : i + 2]) for i in range(0, len(masks_even), 2)]
        for mate in (False, True)
    ]
    early = len(pairs[0]) // 2
    groups = [pairs[0][:early], pairs[0][early:], pairs[1]]
    panel = n_rep * rows
    slots = tiles.shape[1]
    left_sizes = [len(steps) * slots * panel * 2 * rows * 2 for steps in groups]
    prebuilt = sum(left_sizes) <= 4 * 1024 * 1024
    halves = [slice(0, width // 2), slice(width // 2, width)]
    held = [jnp.concatenate([feats[:, half], got[:, half]], axis=0) for half in halves]
    for even, odd in zip(hops[1:-1], turned[1:-1], strict=True):
        gots = [trade(part, (even, 0), (odd, 0)) for part in held]
        gots[0], place, flags, row_ids, live_count = barrier((gots[0], place, flags, row_ids, live_count))
        gots[-1], far = barrier((gots[-1], far))
        held = [jnp.concatenate([part, got], axis=0) for part, got in zip(held, gots, strict=True)]
    tables = [place, row_ids, live_count, tiles]
    table_specs = [SMEM] * 3 + [VMEM]
    gots = [trade(part, (hops[-1], 0), (turned[-1], 0)) for part in held]
    if prebuilt:
        lefts = call(
            functools.partial(build_lefts, sum(groups, [])),
            tuple(jax.ShapeDtypeStruct((len(steps), slots * panel, 2 * rows), BF16) for steps in groups),
            table_specs, 0, 3 * sum(left_sizes),
        )(*tables)
        gots[0], lefts = barrier((gots[0], lefts))

    def sums(indices, columns, seed, dtype):
        steps = [groups[i] for i in indices]
        given, specs = ([lefts[i] for i in indices], [VMEM] * len(indices)) if prebuilt else (tables, table_specs)
        more = columns + ([seed] if seed is not None else [])
        size = sum(left_sizes[i] for i in indices)
        return call(
            functools.partial(tile_sums, steps, prebuilt, len(columns), seed is not None),
            jax.ShapeDtypeStruct((panel, columns[0].shape[1]), dtype),
            specs + [VMEM] * len(more), size * columns[0].shape[1], size,
        )(*given, *more)

    sums_type = BF16 if n_rep == 2 else F32
    first = jnp.concatenate([held[0], gots[0]], axis=0)
    own = sums([0, 1], [first], None, F32)
    gots[1], own = barrier((gots[1], own))
    second = jnp.concatenate([held[1], gots[1]], axis=0)
    total = sums([2], [core_swap(first)], own, sums_type)
    mates = core_swap(second)
    second, total = barrier((second, total))
    totals = [total, sums([0, 1, 2], [second, mates], None, sums_type)]

    gots = []
    for i in (0, 1):
        for bit in rep_bits[:-1]:
            got = trade(totals[i][bit * rows :].astype(BF16), (0, bit), (0, bit))
            totals[i] = totals[i][: bit * rows].astype(F32) + got.astype(F32)
        totals[i] = totals[i].astype(BF16)
        gots.append(trade(totals[i], (0, 1), (0, 1)))

    two_blocks = (2 * rows, width)
    x, aggregate, pre = call(
        update_first,
        (
            jax.ShapeDtypeStruct(two_blocks, BF16),
            jax.ShapeDtypeStruct(totals[0].shape, BF16),
            jax.ShapeDtypeStruct(two_blocks, F32),
        ),
        [VMEM] * 7, 6 * rows * width * width, 1 << 19,
    )(flags, totals[0], gots[0], feats, far[:rows], w_self, w_neigh)
    half_grad = jax.ShapeDtypeStruct((width // 2, width), F32)
    value, keep_top, keep_low, send_top, send_low = call(
        update_second,
        (
            jax.ShapeDtypeStruct((rows, width), BF16), half_grad, half_grad, half_grad, half_grad,
        ),
        [VMEM] * 9, 10 * rows * width * width, 1 << 20,
    )(flags, totals[1], gots[1], x, aggregate, pre, out_grad, far[rows:], w_neigh)
    grads = [keep_top + core_swap(send_top), keep_low + core_swap(send_low)]
    layer_out = call(copied, jax.ShapeDtypeStruct((rows, width), BF16), [VMEM], 0, 4 * rows * width)(value)

    steps = [((0, bit), (0, bit)) for bit in rep_bits[:-1]]
    steps += [((even, 0), (odd, 0)) for even, odd in zip(turned, hops, strict=True)]
    for even, odd in steps[:-1]:
        parts = [grad.astype(BF16) for grad in grads]
        gots = [trade(part, even, odd) for part in parts]
        gots[0], layer_out = barrier((gots[0], layer_out))
        grads = [part.astype(F32) + got.astype(F32) for part, got in zip(parts, gots, strict=True)]
    parts = [grad.astype(BF16) for grad in grads]
    gots = [trade(part, *steps[-1]) for part in parts]
    part, got = jnp.concatenate(parts, axis=0), jnp.concatenate(gots, axis=0)
    other_part = core_swap(part)
    other_got = jnp.concatenate([core_swap(got) for got in gots], axis=0)
    grad = part.astype(F32) + got.astype(F32)
    other_grad = other_part.astype(F32) + other_got.astype(F32)
    first_core = flags[:1] == 0
    grad_self = jnp.where(first_core, grad, other_grad)
    grad_neigh = jnp.where(first_core, other_grad, grad)
    return (layer_out, grad_self, grad_neigh)


def solution(mesh):
    placed = (
        P(("node", "rep"), None),
        P("node", "rep", None, None, None, None),
        P("node", "rep", None, None),
        P("node", "rep", None),
        P(),
        P(),
        P(("node", "rep"), None),
    )
    return jax.shard_map(
        functools.partial(local, mesh.shape["node"], mesh.shape["rep"]),
        mesh=mesh,
        in_specs=placed,
        out_specs=(P(("node", "rep"), None), P(), P()),
        check_vma=False,
    )
```

```python
import functools

import jax
import jax.numpy as jnp
from jax import lax
from jax.experimental import pallas as pl
from jax.experimental.pallas import tpu as pltpu
from jax.sharding import PartitionSpec as P

VMEM = pl.BlockSpec(memory_space=pltpu.VMEM)
SMEM = pl.BlockSpec(memory_space=pltpu.SMEM)
F32 = jnp.float32
BF16 = jnp.bfloat16


def bits_below(size):
    return [1 << i for i in reversed(range(size.bit_length() - 1))]


def doubling_masks(bits):
    masks = [0]
    for bit in bits:
        masks = masks + [mask ^ bit for mask in masks]
    return masks


def swap(x, n_node, n_rep, even, odd):
    pairs = []
    for node in range(n_node):
        flip_node, flip_rep = odd if node.bit_count() & 1 else even
        for rep in range(n_rep):
            pairs.append((node * n_rep + rep, (node ^ flip_node) * n_rep + (rep ^ flip_rep)))
    return lax.ppermute(x, ("node", "rep"), pairs)


def masked_pair(place, rows, count, tiles, out_tiles, mates, even, odd):
    node = place[0]
    base = place[1] - place[3]
    groups = []
    for mate, e, o in zip(mates, even, odd, strict=True):
        origin = node ^ 1 if mate else node
        groups.append(origin ^ jnp.where(place[2] == (0 if mate else 1), o, e))
    lefts = []
    for s in range(tiles.shape[1]):
        for k in range(out_tiles):
            parts = []
            for group in groups:
                live = jnp.logical_and(s < count[group], rows[group * tiles.shape[1] + s] == base ^ k)
                value = tiles[group, s]
                chosen = jnp.full(value.shape, live.astype(F32)) > 0.5
                parts.append(jnp.where(chosen, value, jnp.zeros_like(value)))
            lefts.append(jnp.concatenate(parts, axis=1))
    return jnp.concatenate(lefts, axis=0)


def build_lefts(steps, place, rows, count, tiles, *outs):
    at = 0
    for out in outs:
        for i in range(out.shape[0]):
            out_tiles = out.shape[1] // (tiles.shape[1] * tiles.shape[2])
            out[i] = masked_pair(place, rows, count, tiles, out_tiles, *steps[at])
            at += 1


def tile_sums(groups, prebuilt, n_columns, seeded, *refs):
    refs, out = refs[:-1], refs[-1]
    if seeded:
        refs, seed = refs[:-1], refs[-1]
    refs, columns = refs[:-n_columns], refs[-n_columns:]
    total = seed[...] if seeded else None
    panel = out.shape[0]
    size = sum(part.shape[0] for part in columns) // sum(len(steps) for steps in groups)
    blocks = [part.at[pl.ds(i, size), :] for part in columns for i in range(0, part.shape[0], size)]
    for at, steps in enumerate(groups):
        for i, step in enumerate(steps):
            if prebuilt:
                left = refs[at][i]
            else:
                left = masked_pair(*refs, panel // refs[3].shape[2], *step)
            terms = jnp.dot(left, blocks.pop(0)[...], preferred_element_type=F32)
            for s in range(terms.shape[0] // panel):
                term = terms[s * panel : (s + 1) * panel]
                total = term if total is None else total + term
    out[...] = total.astype(out.dtype)


def summed(total, got):
    return (total[...].astype(F32) + got[...].astype(F32)).astype(BF16)


def flag_like(flags, i, x):
    return jnp.broadcast_to(flags[i : i + 1, : x.shape[1]], x.shape) == 0


def in_order(flags, mine, far):
    first_rep = flag_like(flags, 1, mine)
    return jnp.concatenate(
        [jnp.where(first_rep, mine[...], far[...]), jnp.where(first_rep, far[...], mine[...])], axis=0
    )


def update_first(flags, total, got, feats, far_feats, w_self, w_neigh, x, aggregate, pre):
    x[...] = in_order(flags, feats, far_feats)
    aggregate[...] = summed(total, got)
    pre[...] = jnp.dot(x[...], w_self[...], preferred_element_type=F32) + jnp.dot(
        aggregate[...], w_neigh[: aggregate.shape[1], :], preferred_element_type=F32
    )


def update_second(flags, total, got, x, first_aggregate, first_pre, out_grad, far_out_grad, w_neigh, *outs):
    value, keep_top, keep_low, send_top, send_low = outs
    rows, split = out_grad.shape[0], first_aggregate.shape[1]
    second_aggregate = summed(total, got)
    aggregate = jnp.concatenate([first_aggregate[...], second_aggregate], axis=1)
    pre = first_pre[...] + jnp.dot(second_aggregate, w_neigh[split:, :], preferred_element_type=F32)
    sigma = jax.nn.sigmoid(pre)
    both = (pre * sigma).astype(BF16)
    value[...] = jnp.where(flag_like(flags, 1, value), both[:rows], both[rows:])
    g = in_order(flags, out_grad, far_out_grad).astype(F32)
    delta = (g * sigma * (1.0 + pre * (1.0 - sigma))).astype(BF16)
    first_core = flag_like(flags, 0, x)
    for left, top, low in (
        (jnp.where(first_core, aggregate, x[...]), send_top, send_low),
        (jnp.where(first_core, x[...], aggregate), keep_top, keep_low),
    ):
        grad = lax.dot_general(left, delta, (((0,), (0,)), ((), ())), preferred_element_type=F32)
        top[...] = grad[: top.shape[0]]
        low[...] = grad[top.shape[0] :]


def copied(x_ref, out_ref):
    out_ref[...] = x_ref[...]


def call(body, out_shape, specs, flops, nbytes):
    return pl.pallas_call(
        body,
        out_shape=out_shape,
        in_specs=specs,
        out_specs=jax.tree.map(lambda _: VMEM, out_shape),
        cost_estimate=pl.CostEstimate(flops=flops, bytes_accessed=nbytes, transcendentals=0),
        compiler_params=pltpu.CompilerParams(vmem_limit_bytes=24 * 1024 * 1024),
    )


def local(n_node, n_rep, node_feats, tile_vals, tile_rows, tile_count, w_self, w_neigh, out_grad):
    tiles = tile_vals[0, 0]
    rows, width = node_feats.shape
    node, rep = lax.axis_index("node"), lax.axis_index("rep")
    barrier = lax.optimization_barrier

    bits = [bit | 1 for bit in bits_below(n_node)[:-1]]
    hops, turned = bits[:1] + bits[2:] + bits[1:2], bits[1:2] + bits[:1] + bits[2:]
    rep_bits = bits_below(n_rep)

    def trade(x, even, odd):
        return swap(x, n_node, n_rep, even, odd)

    def core_swap(x):
        return trade(x, (1, 0), (1, 0))

    got = trade(node_feats, (hops[0], 0), (turned[0], 0))
    feats = call(copied, jax.ShapeDtypeStruct(node_feats.shape, BF16), [VMEM], 0, node_feats.size * 4)(node_feats)
    far = trade(jnp.concatenate([feats, out_grad], axis=0), (0, 1), (0, 1))
    row_ids = tile_rows[0, 0].reshape(-1)
    feats, got, tables = barrier((feats, got, (node, rep, row_ids, tile_count)))
    node, rep, row_ids, tile_count = tables
    live_count = tile_count[0, 0]
    parity = node
    for shift in reversed(range((n_node.bit_length() - 2).bit_length())):
        parity = parity ^ (parity >> (1 << shift))
    place = jnp.stack([node, rep, parity & 1, rep & 1]).astype(jnp.int32)
    flags = jnp.broadcast_to(place[2:, None], (2, width))
    masks_even, masks_odd = doubling_masks(hops), doubling_masks(turned)
    pairs = [
        [((mate, mate), masks_even[i : i + 2], masks_odd[i : i + 2]) for i in range(0, len(masks_even), 2)]
        for mate in (False, True)
    ]
    early = len(pairs[0]) // 2
    groups = [pairs[0][:early], pairs[0][early:], pairs[1]]
    panel = n_rep * rows
    slots = tiles.shape[1]
    left_sizes = [len(steps) * slots * panel * 2 * rows * 2 for steps in groups]
    prebuilt = sum(left_sizes) <= 4 * 1024 * 1024
    halves = [slice(0, width // 2), slice(width // 2, width)]
    held = [jnp.concatenate([feats[:, half], got[:, half]], axis=0) for half in halves]
    for even, odd in zip(hops[1:-1], turned[1:-1], strict=True):
        gots = [trade(part, (even, 0), (odd, 0)) for part in held]
        gots[0], place, flags, row_ids, live_count = barrier((gots[0], place, flags, row_ids, live_count))
        gots[0], far = barrier((gots[0], far))
        held = [jnp.concatenate([part, got], axis=0) for part, got in zip(held, gots, strict=True)]
    tables = [place, row_ids, live_count, tiles]
    table_specs = [SMEM] * 3 + [VMEM]
    gots = [trade(part, (hops[-1], 0), (turned[-1], 0)) for part in held]
    if prebuilt:
        lefts = call(
            functools.partial(build_lefts, sum(groups, [])),
            tuple(jax.ShapeDtypeStruct((len(steps), slots * panel, 2 * rows), BF16) for steps in groups),
            table_specs, 0, 3 * sum(left_sizes),
        )(*tables)
        gots[0], lefts = barrier((gots[0], lefts))

    def sums(indices, columns, seed, dtype):
        steps = [groups[i] for i in indices]
        given, specs = ([lefts[i] for i in indices], [VMEM] * len(indices)) if prebuilt else (tables, table_specs)
        more = columns + ([seed] if seed is not None else [])
        size = sum(left_sizes[i] for i in indices)
        return call(
            functools.partial(tile_sums, steps, prebuilt, len(columns), seed is not None),
            jax.ShapeDtypeStruct((panel, columns[0].shape[1]), dtype),
            specs + [VMEM] * len(more), size * columns[0].shape[1], size,
        )(*given, *more)

    sums_type = BF16 if n_rep == 2 else F32
    first = jnp.concatenate([held[0], gots[0]], axis=0)
    own = sums([0, 1], [first], None, F32)
    gots[1], own = barrier((gots[1], own))
    second = jnp.concatenate([held[1], gots[1]], axis=0)
    total = sums([2], [core_swap(first)], own, sums_type)
    mates = core_swap(second)
    second, total = barrier((second, total))
    totals = [total, sums([0, 1, 2], [second, mates], None, sums_type)]

    gots = []
    for i in (0, 1):
        for bit in rep_bits[:-1]:
            got = trade(totals[i][bit * rows :].astype(BF16), (0, bit), (0, bit))
            totals[i] = totals[i][: bit * rows].astype(F32) + got.astype(F32)
        totals[i] = totals[i].astype(BF16)
        gots.append(trade(totals[i], (0, 1), (0, 1)))

    two_blocks = (2 * rows, width)
    x, aggregate, pre = call(
        update_first,
        (
            jax.ShapeDtypeStruct(two_blocks, BF16),
            jax.ShapeDtypeStruct(totals[0].shape, BF16),
            jax.ShapeDtypeStruct(two_blocks, F32),
        ),
        [VMEM] * 7, 6 * rows * width * width, 1 << 19,
    )(flags, totals[0], gots[0], feats, far[:rows], w_self, w_neigh)
    half_grad = jax.ShapeDtypeStruct((width // 2, width), F32)
    value, keep_top, keep_low, send_top, send_low = call(
        update_second,
        (
            jax.ShapeDtypeStruct((rows, width), BF16), half_grad, half_grad, half_grad, half_grad,
        ),
        [VMEM] * 9, 10 * rows * width * width, 1 << 20,
    )(flags, totals[1], gots[1], x, aggregate, pre, out_grad, far[rows:], w_neigh)
    grads = [keep_top + core_swap(send_top), keep_low + core_swap(send_low)]
    layer_out = call(copied, jax.ShapeDtypeStruct((rows, width), BF16), [VMEM], 0, 4 * rows * width)(value)

    steps = [((0, bit), (0, bit)) for bit in rep_bits[:-1]]
    steps += [((even, 0), (odd, 0)) for even, odd in zip(turned, hops, strict=True)]
    for even, odd in steps[:-1]:
        parts = [grad.astype(BF16) for grad in grads]
        gots = [trade(part, even, odd) for part in parts]
        gots[0], layer_out = barrier((gots[0], layer_out))
        grads = [part.astype(F32) + got.astype(F32) for part, got in zip(parts, gots, strict=True)]
    parts = [grad.astype(BF16) for grad in grads]
    gots = [trade(part, *steps[-1]) for part in parts]
    part, got = jnp.concatenate(parts, axis=0), jnp.concatenate(gots, axis=0)
    other_part = core_swap(part)
    other_got = jnp.concatenate([core_swap(got) for got in gots], axis=0)
    grad = part.astype(F32) + got.astype(F32)
    other_grad = other_part.astype(F32) + other_got.astype(F32)
    first_core = flags[:1] == 0
    grad_self = jnp.where(first_core, grad, other_grad)
    grad_neigh = jnp.where(first_core, other_grad, grad)
    return (layer_out, grad_self, grad_neigh)


def solution(mesh):
    placed = (
        P(("node", "rep"), None),
        P("node", "rep", None, None, None, None),
        P("node", "rep", None, None),
        P("node", "rep", None),
        P(),
        P(),
        P(("node", "rep"), None),
    )
    return jax.shard_map(
        functools.partial(local, mesh.shape["node"], mesh.shape["rep"]),
        mesh=mesh,
        in_specs=placed,
        out_specs=(P(("node", "rep"), None), P(), P()),
        check_vma=False,
    )
```

```python
import functools

import jax
import jax.numpy as jnp
from jax import lax
from jax.experimental import pallas as pl
from jax.experimental.pallas import tpu as pltpu
from jax.sharding import PartitionSpec as P

VMEM = pl.BlockSpec(memory_space=pltpu.VMEM)
SMEM = pl.BlockSpec(memory_space=pltpu.SMEM)
F32 = jnp.float32
BF16 = jnp.bfloat16


def bits_below(size):
    return [1 << i for i in reversed(range(size.bit_length() - 1))]


def doubling_masks(bits):
    masks = [0]
    for bit in bits:
        masks = masks + [mask ^ bit for mask in masks]
    return masks


def swap(x, n_node, n_rep, even, odd):
    pairs = []
    for node in range(n_node):
        flip_node, flip_rep = odd if node.bit_count() & 1 else even
        for rep in range(n_rep):
            pairs.append((node * n_rep + rep, (node ^ flip_node) * n_rep + (rep ^ flip_rep)))
    return lax.ppermute(x, ("node", "rep"), pairs)


def masked_pair(place, rows, count, tiles, out_tiles, mates, even, odd):
    node = place[0]
    base = place[1] - place[3]
    groups = []
    for mate, e, o in zip(mates, even, odd, strict=True):
        origin = node ^ 1 if mate else node
        groups.append(origin ^ jnp.where(place[2] == (0 if mate else 1), o, e))
    lefts = []
    for s in range(tiles.shape[1]):
        for k in range(out_tiles):
            parts = []
            for group in groups:
                live = jnp.logical_and(s < count[group], rows[group * tiles.shape[1] + s] == base ^ k)
                value = tiles[group, s]
                chosen = jnp.full(value.shape, live.astype(F32)) > 0.5
                parts.append(jnp.where(chosen, value, jnp.zeros_like(value)))
            lefts.append(jnp.concatenate(parts, axis=1))
    return jnp.concatenate(lefts, axis=0)


def build_lefts(steps, place, rows, count, tiles, *outs):
    at = 0
    for out in outs:
        for i in range(out.shape[0]):
            out_tiles = out.shape[1] // (tiles.shape[1] * tiles.shape[2])
            out[i] = masked_pair(place, rows, count, tiles, out_tiles, *steps[at])
            at += 1


def tile_sums(groups, prebuilt, n_columns, seeded, *refs):
    refs, out = refs[:-1], refs[-1]
    if seeded:
        refs, seed = refs[:-1], refs[-1]
    refs, columns = refs[:-n_columns], refs[-n_columns:]
    total = seed[...] if seeded else None
    panel = out.shape[0]
    size = sum(part.shape[0] for part in columns) // sum(len(steps) for steps in groups)
    blocks = [part.at[pl.ds(i, size), :] for part in columns for i in range(0, part.shape[0], size)]
    for at, steps in enumerate(groups):
        for i, step in enumerate(steps):
            if prebuilt:
                left = refs[at][i]
            else:
                left = masked_pair(*refs, panel // refs[3].shape[2], *step)
            terms = jnp.dot(left, blocks.pop(0)[...], preferred_element_type=F32)
            for s in range(terms.shape[0] // panel):
                term = terms[s * panel : (s + 1) * panel]
                total = term if total is None else total + term
    out[...] = total.astype(out.dtype)


def summed(total, got):
    return (total[...].astype(F32) + got[...].astype(F32)).astype(BF16)


def flag_like(flags, i, x):
    return jnp.broadcast_to(flags[i : i + 1, : x.shape[1]], x.shape) == 0


def in_order(flags, mine, far):
    first_rep = flag_like(flags, 1, mine)
    return jnp.concatenate(
        [jnp.where(first_rep, mine[...], far[...]), jnp.where(first_rep, far[...], mine[...])], axis=0
    )


def update_first(flags, total, got, feats, far_feats, w_self, w_neigh, x, aggregate, pre):
    x[...] = in_order(flags, feats, far_feats)
    aggregate[...] = summed(total, got)
    pre[...] = jnp.dot(x[...], w_self[...], preferred_element_type=F32) + jnp.dot(
        aggregate[...], w_neigh[: aggregate.shape[1], :], preferred_element_type=F32
    )


def update_second(flags, total, got, x, first_aggregate, first_pre, out_grad, far_out_grad, w_neigh, *outs):
    value, keep_top, keep_low, send_top, send_low = outs
    rows, split = out_grad.shape[0], first_aggregate.shape[1]
    second_aggregate = summed(total, got)
    aggregate = jnp.concatenate([first_aggregate[...], second_aggregate], axis=1)
    pre = first_pre[...] + jnp.dot(second_aggregate, w_neigh[split:, :], preferred_element_type=F32)
    sigma = jax.nn.sigmoid(pre)
    both = (pre * sigma).astype(BF16)
    value[...] = jnp.where(flag_like(flags, 1, value), both[:rows], both[rows:])
    g = in_order(flags, out_grad, far_out_grad).astype(F32)
    delta = (g * sigma * (1.0 + pre * (1.0 - sigma))).astype(BF16)
    first_core = flag_like(flags, 0, x)
    for left, top, low in (
        (jnp.where(first_core, aggregate, x[...]), send_top, send_low),
        (jnp.where(first_core, x[...], aggregate), keep_top, keep_low),
    ):
        grad = lax.dot_general(left, delta, (((0,), (0,)), ((), ())), preferred_element_type=F32)
        top[...] = grad[: top.shape[0]]
        low[...] = grad[top.shape[0] :]


def copied(x_ref, out_ref):
    out_ref[...] = x_ref[...]


def call(body, out_shape, specs, flops, nbytes):
    return pl.pallas_call(
        body,
        out_shape=out_shape,
        in_specs=specs,
        out_specs=jax.tree.map(lambda _: VMEM, out_shape),
        cost_estimate=pl.CostEstimate(flops=flops, bytes_accessed=nbytes, transcendentals=0),
        compiler_params=pltpu.CompilerParams(vmem_limit_bytes=24 * 1024 * 1024),
    )


def local(n_node, n_rep, node_feats, tile_vals, tile_rows, tile_count, w_self, w_neigh, out_grad):
    tiles = tile_vals[0, 0]
    rows, width = node_feats.shape
    node, rep = lax.axis_index("node"), lax.axis_index("rep")
    barrier = lax.optimization_barrier

    bits = [bit | 1 for bit in bits_below(n_node)[:-1]]
    hops, turned = bits[:1] + bits[2:] + bits[1:2], bits[1:2] + bits[:1] + bits[2:]
    rep_bits = bits_below(n_rep)

    def trade(x, even, odd):
        return swap(x, n_node, n_rep, even, odd)

    def core_swap(x):
        return trade(x, (1, 0), (1, 0))

    got = trade(node_feats, (hops[0], 0), (turned[0], 0))
    feats = call(copied, jax.ShapeDtypeStruct(node_feats.shape, BF16), [VMEM], 0, node_feats.size * 4)(node_feats)
    far = trade(jnp.concatenate([feats, out_grad], axis=0), (0, 1), (0, 1))
    row_ids = tile_rows[0, 0].reshape(-1)
    feats, got, tables = barrier((feats, got, (node, rep, row_ids, tile_count)))
    node, rep, row_ids, tile_count = tables
    live_count = tile_count[0, 0]
    parity = node
    for shift in reversed(range((n_node.bit_length() - 2).bit_length())):
        parity = parity ^ (parity >> (1 << shift))
    place = jnp.stack([node, rep, parity & 1, rep & 1]).astype(jnp.int32)
    flags = jnp.broadcast_to(place[2:, None], (2, width))
    masks_even, masks_odd = doubling_masks(hops), doubling_masks(turned)
    pairs = [
        [((mate, mate), masks_even[i : i + 2], masks_odd[i : i + 2]) for i in range(0, len(masks_even), 2)]
        for mate in (False, True)
    ]
    early = len(pairs[0]) // 2
    groups = [pairs[0][:early], pairs[0][early:], pairs[1]]
    panel = n_rep * rows
    slots = tiles.shape[1]
    left_sizes = [len(steps) * slots * panel * 2 * rows * 2 for steps in groups]
    prebuilt = sum(left_sizes) <= 4 * 1024 * 1024
    halves = [slice(0, width // 2), slice(width // 2, width)]
    held = [jnp.concatenate([feats[:, half], got[:, half]], axis=0) for half in halves]
    for even, odd in zip(hops[1:-1], turned[1:-1], strict=True):
        gots = [trade(part, (even, 0), (odd, 0)) for part in held]
        gots[0], place, flags, row_ids, live_count = barrier((gots[0], place, flags, row_ids, live_count))
        gots[0], far = barrier((gots[0], far))
        held = [jnp.concatenate([part, got], axis=0) for part, got in zip(held, gots, strict=True)]
    tables = [place, row_ids, live_count, tiles]
    table_specs = [SMEM] * 3 + [VMEM]
    gots = [trade(part, (hops[-1], 0), (turned[-1], 0)) for part in held]
    if prebuilt:
        lefts = call(
            functools.partial(build_lefts, sum(groups, [])),
            tuple(jax.ShapeDtypeStruct((len(steps), slots * panel, 2 * rows), BF16) for steps in groups),
            table_specs, 0, 3 * sum(left_sizes),
        )(*tables)
        gots[0], lefts = barrier((gots[0], lefts))

    def sums(indices, columns, seed, dtype):
        steps = [groups[i] for i in indices]
        given, specs = ([lefts[i] for i in indices], [VMEM] * len(indices)) if prebuilt else (tables, table_specs)
        more = columns + ([seed] if seed is not None else [])
        size = sum(left_sizes[i] for i in indices)
        return call(
            functools.partial(tile_sums, steps, prebuilt, len(columns), seed is not None),
            jax.ShapeDtypeStruct((panel, columns[0].shape[1]), dtype),
            specs + [VMEM] * len(more), size * columns[0].shape[1], size,
        )(*given, *more)

    sums_type = BF16 if n_rep == 2 else F32
    first = jnp.concatenate([held[0], gots[0]], axis=0)
    own = sums([0, 1], [first], None, F32)
    gots[1], own = barrier((gots[1], own))
    second = jnp.concatenate([held[1], gots[1]], axis=0)
    total = sums([2], [core_swap(first)], own, sums_type)
    mates = core_swap(second)
    second, total = barrier((second, total))
    totals = [total, sums([0, 1, 2], [second, mates], None, sums_type)]

    gots = []
    for i in (0, 1):
        for bit in rep_bits[:-1]:
            got = trade(totals[i][bit * rows :].astype(BF16), (0, bit), (0, bit))
            totals[i] = totals[i][: bit * rows].astype(F32) + got.astype(F32)
        totals[i] = totals[i].astype(BF16)
        gots.append(trade(totals[i], (0, 1), (0, 1)))

    two_blocks = (2 * rows, width)
    x, aggregate, pre = call(
        update_first,
        (
            jax.ShapeDtypeStruct(two_blocks, BF16),
            jax.ShapeDtypeStruct(totals[0].shape, BF16),
            jax.ShapeDtypeStruct(two_blocks, F32),
        ),
        [VMEM] * 7, 6 * rows * width * width, 1 << 19,
    )(flags, totals[0], gots[0], feats, far[:rows], w_self, w_neigh)
    half_grad = jax.ShapeDtypeStruct((width // 2, width), F32)
    value, keep_top, keep_low, send_top, send_low = call(
        update_second,
        (
            jax.ShapeDtypeStruct((rows, width), BF16), half_grad, half_grad, half_grad, half_grad,
        ),
        [VMEM] * 9, 10 * rows * width * width, 1 << 20,
    )(flags, totals[1], gots[1], x, aggregate, pre, out_grad, far[rows:], w_neigh)
    grads = [keep_top + core_swap(send_top), keep_low + core_swap(send_low)]
    layer_out = call(copied, jax.ShapeDtypeStruct((rows, width), BF16), [VMEM], 0, 4 * rows * width)(value)

    steps = [((0, bit), (0, bit)) for bit in rep_bits[:-1]]
    steps += [((even, 0), (odd, 0)) for even, odd in zip(turned, hops, strict=True)]
    for at, (even, odd) in enumerate(steps[:-1]):
        parts = [grad.astype(BF16) for grad in grads]
        gots = [trade(part, even, odd) for part in parts]
        if at == 1:
            gots[0], layer_out = barrier((gots[0], layer_out))
        grads = [part.astype(F32) + got.astype(F32) for part, got in zip(parts, gots, strict=True)]
    parts = [grad.astype(BF16) for grad in grads]
    gots = [trade(part, *steps[-1]) for part in parts]
    part, got = jnp.concatenate(parts, axis=0), jnp.concatenate(gots, axis=0)
    other_part = core_swap(part)
    other_got = jnp.concatenate([core_swap(got) for got in gots], axis=0)
    grad = part.astype(F32) + got.astype(F32)
    other_grad = other_part.astype(F32) + other_got.astype(F32)
    first_core = flags[:1] == 0
    grad_self = jnp.where(first_core, grad, other_grad)
    grad_neigh = jnp.where(first_core, other_grad, grad)
    return (layer_out, grad_self, grad_neigh)


def solution(mesh):
    placed = (
        P(("node", "rep"), None),
        P("node", "rep", None, None, None, None),
        P("node", "rep", None, None),
        P("node", "rep", None),
        P(),
        P(),
        P(("node", "rep"), None),
    )
    return jax.shard_map(
        functools.partial(local, mesh.shape["node"], mesh.shape["rep"]),
        mesh=mesh,
        in_specs=placed,
        out_specs=(P(("node", "rep"), None), P(), P()),
        check_vma=False,
    )
```
